32 devices in a mesh: groups: 2 (over y), chan: 16 (over z, x, core).
Axes of the slice: x: 2, y: 2, z: 4, core: 2. Of those that a mesh axis runs over, the one named last changes fastest.
Arguments:
- eta: bfloat16 [16384, 512], P(('groups', 'chan')), parts along dimension 0, as said below
- ham: bfloat16 [16384, 512], P(('groups', 'chan')), parts along dimension 0, as said below
- pp_occ: int32 [32, 2, 512], P(('groups', 'chan')), parts along dimension 0, may hold values 0 or 1
- ph_occ: int32 [32, 2, 512], P(('groups', 'chan')), parts along dimension 0, may hold values 0 or 1
- ph_src: int32 [32, 16, 8], P(('groups', 'chan')), parts along dimension 0, may hold values from 0 to 255, as said below
- coef6j: float32 [32, 16, 8], P(('groups', 'chan')), parts along dimension 0, may hold values from -1 to 1
Outputs:
- flow: float32 [16384, 512], P(('groups', 'chan')), parts along dimension 0
The draws below stay inside these ranges and needn't reach their ends.
There are 2 independent parts, one for each index of `groups`. The reference program is written for one: setup_inputs(seed, part) draws one part's arguments, and reference() takes and returns one part's arrays. A program takes and returns all parts, laid end to end along the dimension named above; each array names one. Nothing has to cross between parts.
Inputs may be any that keep to these rules, and one draw needn't show every extreme that they name: eta is antisymmetric and ham symmetric within each channel's 512 x 512 block. ham is symmetric within each channel's block. ph_src names pp block g = c * 16 + b; within one ph channel no block is named twice, and every pp channel that it names gives exactly 8 of its blocks.
All inputs are finite; a program needn't handle non-finite values. No bound on the sum of `pp_occ` or of `ph_occ` on one device may be relied on, other than what follows from the above.
Results may differ from the reference program's by a relative error of at most 0.0048.
Values may be sent and summed in bfloat16 or wider, within the bound.
A program may use at most 128 MiB of HBM per device.

```python
import jax
import jax.numpy as jnp
from jax import lax

B = 128
NBR = 4
K = 8
M = 512
NBLK = 16
CHANNELS = 16
CAP = 8


def noise_field(key):
    return jax.random.normal(key, (CHANNELS, M, M), jnp.float32)


def draw_eta(key, part):
    key = jax.random.fold_in(key, 3)
    noise = noise_field(key)
    result = (noise - jnp.swapaxes(noise, 1, 2)) / jnp.sqrt(2.0 * M)
    return result.reshape(CHANNELS * M, M).astype(jnp.bfloat16)


def draw_ham(key, part):
    key = jax.random.fold_in(key, 5)
    noise = noise_field(key)
    result = (noise + jnp.swapaxes(noise, 1, 2)) / jnp.sqrt(2.0)
    return result.reshape(CHANNELS * M, M).astype(jnp.bfloat16)


def draw_ph_src(key, part):
    key = jax.random.fold_in(key, 11)
    used = NBLK * K // CAP

    def pick_blocks(block_key):
        return jax.random.permutation(block_key, NBLK)[:CAP]

    def one_channel(chan_key):
        key_src = jax.random.fold_in(chan_key, 1)
        key_blk = jax.random.fold_in(chan_key, 2)
        key_ord = jax.random.fold_in(chan_key, 3)
        sources = jax.random.permutation(key_src, CHANNELS)[:used]
        blocks = jax.vmap(pick_blocks)(jax.random.split(key_blk, used))
        ref_list = (sources[:, None] * NBLK + blocks).reshape(NBLK * K)
        shuffle = jax.random.permutation(key_ord, NBLK * K)
        return ref_list[shuffle].reshape(NBLK, K).astype(jnp.int32)
    return jax.vmap(one_channel)(jax.random.split(key, CHANNELS))


def plant(values, stream_key, low, largest):
    shape = values.shape
    place = [jax.random.randint(jax.random.fold_in(stream_key, axis), (), 0, shape[axis]) for axis in range(len(shape))]
    values = values.at[tuple(place)].set(low)
    longest = shape.index(max(shape))
    place[longest] = (place[longest] + 1) % shape[longest]
    return values.at[tuple(place)].set(largest)


def level_of(key, dims, cuts, least, largest):
    loudness = 1.0
    for dim, shards_of in cuts:
        steps = jax.random.uniform(jax.random.fold_in(jax.random.fold_in(key, 6), dim), (shards_of,), jnp.float32, least / len(cuts), largest / len(cuts))
        loudness = loudness * jnp.repeat(jnp.exp(steps), dims[dim] // shards_of).reshape((-1,) + (1,) * (len(dims) - 1 - dim))
    return loudness


def setup_inputs(seed: int = 0, part: int = 0) -> dict:
    streams_of = jax.random.split(jax.random.key(seed), 7)
    part_keys = jax.random.split(jax.random.fold_in(streams_of[6], part), 7)
    return {
        "eta": draw_eta(jax.random.fold_in(jax.random.fold_in(streams_of[6], part), 71), part),
        "ham": draw_ham(jax.random.fold_in(jax.random.fold_in(streams_of[6], part), 71), part),
        "pp_occ": plant((jax.random.randint(part_keys[2], (CHANNELS, 2, M), 0, 3) < 1).astype(jnp.int32), jax.random.fold_in(part_keys[2], 1), 0, 1),
        "ph_occ": plant((jax.random.randint(part_keys[3], (CHANNELS, 2, M), 0, 3) < 1).astype(jnp.int32), jax.random.fold_in(part_keys[3], 1), 0, 1),
        "ph_src": draw_ph_src(jax.random.fold_in(jax.random.fold_in(streams_of[6], part), 71), part),
        "coef6j": jnp.clip(jax.random.uniform(part_keys[5], (CHANNELS, NBLK, K), jnp.float32, -1.0, 1.0) * level_of(part_keys[5], (CHANNELS, NBLK, K), ((0, 16),), -0.4, 0.0), -1.0, 1.0),
    }


def to_tiles(matrix):
    return matrix.reshape(CHANNELS, NBR, B, NBR, B).transpose(0, 1, 3, 2, 4).reshape(CHANNELS * NBLK, B, B)


def from_tiles(tiles):
    return tiles.reshape(CHANNELS, NBR, NBR, B, B).transpose(0, 1, 3, 2, 4).reshape(CHANNELS * M, M)


def join_tiles(tiles):
    return tiles.reshape(NBR, NBR, B, B).transpose(0, 2, 1, 3).reshape(M, M)


def split_tiles(matrix):
    return matrix.reshape(NBR, B, NBR, B).transpose(0, 2, 1, 3).reshape(NBLK, B, B)


def reference(eta, ham, pp_occ, ph_occ, ph_src, coef6j):
    eta_tiles = to_tiles(eta)
    ham_tiles = to_tiles(ham)

    def recouple(accum, inputs):
        ref_table, weight_table, occ_row = inputs
        flat_refs = ref_table.reshape(NBLK * K)
        scale = weight_table.reshape(NBLK, K, 1, 1)
        mix_eta = jnp.zeros((NBLK, B, B), jnp.float32)
        mix_ham = jnp.zeros((NBLK, B, B), jnp.float32)
        for term in range(K):
            refs = ref_table[:, term]
            mix_eta = mix_eta + eta_tiles[refs].astype(jnp.float32) * scale[:, term]
            mix_ham = mix_ham + ham_tiles[refs].astype(jnp.float32) * scale[:, term]
        mat_eta = join_tiles(mix_eta.astype(jnp.bfloat16))
        mat_ham = join_tiles(mix_ham.astype(jnp.bfloat16))
        occ_ph = (occ_row[0] - occ_row[1]).astype(jnp.bfloat16)
        z_matrix = jnp.dot(mat_eta * occ_ph[None, :], mat_ham, preferred_element_type=jnp.float32) - jnp.dot(mat_ham * occ_ph[None, :], mat_eta, preferred_element_type=jnp.float32)
        z_tiles = split_tiles(z_matrix).reshape(NBLK, 1, B, B)
        back_terms = (z_tiles * scale).astype(jnp.bfloat16).reshape(NBLK * K, B, B)
        accum = accum.at[flat_refs].add(back_terms.astype(jnp.float32))
        return accum, None

    start = jnp.zeros((CHANNELS * NBLK, B, B), jnp.float32)
    accum, _ = lax.scan(recouple, start, (ph_src, coef6j, ph_occ))

    def ladder_one(inputs):
        eta_one, ham_one, occ_row = inputs
        occ_pp = (1 - occ_row[0] - occ_row[1]).astype(jnp.bfloat16)
        return jnp.dot(eta_one * occ_pp[None, :], ham_one, preferred_element_type=jnp.float32) - jnp.dot(ham_one * occ_pp[None, :], eta_one, preferred_element_type=jnp.float32)

    ladder = lax.map(ladder_one, (eta.reshape(CHANNELS, M, M), ham.reshape(CHANNELS, M, M), pp_occ))
    return ladder.reshape(CHANNELS * M, M) + from_tiles(accum)
```

```python
import functools

import jax
import jax.numpy as jnp
from jax import lax
from jax.experimental import pallas as pl
from jax.experimental.pallas import tpu as pltpu
from jax.sharding import PartitionSpec as P

B = 128
NBR = 4
K = 8
NBLK = 16
TERMS = NBLK * K
MESH = pl.DeviceIdType.MESH
LIMIT = 48 * 1024 * 1024


def exchange_plan(eta, ham, pp_occ, ph_occ, ph_src, coef6j):
    chan_count = lax.axis_size("chan")
    chan_order = eta.shape[0]
    tile_size = B
    row_tiles = NBR
    tile_count = NBLK
    term_count = tile_count * K
    capacity = max(2, term_count // chan_count)

    def split_tiles(matrix):
        return (
            matrix.reshape(row_tiles, tile_size, row_tiles, tile_size)
            .transpose(0, 2, 1, 3)
            .reshape(tile_count, tile_size, tile_size)
        )

    def join_tiles(tiles):
        return (
            tiles.reshape(row_tiles, row_tiles, tile_size, tile_size)
            .transpose(0, 2, 1, 3)
            .reshape(chan_order, chan_order)
        )

    ref_list = ph_src.reshape(term_count)
    source = ref_list // tile_count
    within = ref_list % tile_count
    lane_ids = jnp.arange(chan_count, dtype=jnp.int32)
    hit_table = (source[:, None] == lane_ids[None, :]).astype(jnp.int32)
    slot_of = jnp.sum(jnp.cumsum(hit_table, axis=0) * hit_table, axis=1) - 1
    place_at = source * capacity + slot_of
    wanted = (
        jnp.full((chan_count * capacity,), -1, jnp.int32)
        .at[place_at]
        .set(within)
        .reshape(chan_count, capacity)
    )
    asked_for = lax.all_to_all(wanted, "chan", split_axis=0, concat_axis=0, tiled=True)
    weights = coef6j.reshape(tile_count, K)
    live = (asked_for >= 0)[:, :, None, None]
    safe_ids = jnp.maximum(asked_for, 0)

    def mix_terms(picked):
        shaped = picked.reshape(tile_count, K, tile_size, tile_size)
        total = jnp.zeros((tile_count, tile_size, tile_size), jnp.float32)
        for term in range(K):
            total = total + shaped[:, term].astype(jnp.float32) * weights[:, term][:, None, None]
        return join_tiles(total.astype(jnp.bfloat16))

    eta_tiles = split_tiles(eta)
    ham_tiles = split_tiles(ham)
    pair_blocks = jnp.stack([eta_tiles, ham_tiles], axis=1)
    outgoing = jnp.where(live[:, :, None], pair_blocks[safe_ids], jnp.zeros((), jnp.bfloat16))
    incoming = lax.all_to_all(outgoing, "chan", split_axis=0, concat_axis=0, tiled=True)
    picked = incoming.reshape(chan_count * capacity, 2, tile_size, tile_size)[place_at]
    ph_eta = mix_terms(picked[:, 0])
    ph_ham = mix_terms(picked[:, 1])
    occ_ph = (ph_occ[0, 0] - ph_occ[0, 1]).astype(jnp.bfloat16)
    z_matrix = jnp.dot(
        ph_eta * occ_ph[None, :], ph_ham, preferred_element_type=jnp.float32
    ) - jnp.dot(ph_ham * occ_ph[None, :], ph_eta, preferred_element_type=jnp.float32)
    back_terms = (
        (split_tiles(z_matrix)[:, None] * weights[:, :, None, None])
        .astype(jnp.bfloat16)
        .reshape(term_count, tile_size, tile_size)
    )
    outgoing_back = (
        jnp.zeros((chan_count * capacity, tile_size, tile_size), jnp.bfloat16)
        .at[place_at]
        .set(back_terms)
        .reshape(chan_count, capacity, tile_size, tile_size)
    )
    returned = lax.all_to_all(outgoing_back, "chan", split_axis=0, concat_axis=0, tiled=True)
    tile_ids = jnp.arange(tile_count, dtype=jnp.int32)
    selector = (asked_for.reshape(chan_count * capacity)[None, :] == tile_ids[:, None]).astype(
        jnp.bfloat16
    )
    ph_term = jnp.dot(
        selector,
        returned.reshape(chan_count * capacity, tile_size * tile_size),
        preferred_element_type=jnp.float32,
    ).reshape(tile_count, tile_size, tile_size)
    occ_pp = (1 - pp_occ[0, 0] - pp_occ[0, 1]).astype(jnp.bfloat16)
    ladder = jnp.dot(eta * occ_pp[None, :], ham, preferred_element_type=jnp.float32) - jnp.dot(
        ham * occ_pp[None, :], eta, preferred_element_type=jnp.float32
    )
    return ladder + join_tiles(ph_term)


LEVELS = 4


def gather_kernel(eta_ref, ham_ref, occ_ref, all_ref, ladder_ref, mine, send_z, send_x, send_c, recv, local):
    group = lax.axis_index("groups")
    me = lax.axis_index("chan")
    level = me // 4
    side = (me // 2) % 2
    core = me % 2

    def chan_at(lvl, sd, cr):
        return (lvl * 2 + sd) * 2 + cr

    up = chan_at(level + 1, side, core)
    down = chan_at(level - 1, side, core)
    across = chan_at(level, 1 - side, core)
    twin = chan_at(level, side, 1 - core)
    has_up = level < LEVELS - 1
    has_down = level > 0

    barrier = pltpu.get_barrier_semaphore()

    def greet(target):
        pl.semaphore_signal(barrier, inc=1, device_id=(group, target), device_id_type=MESH)

    greet(across)
    greet(twin)

    @pl.when(has_up)
    def _():
        greet(up)

    @pl.when(has_down)
    def _():
        greet(down)

    rows = lax.broadcasted_iota(jnp.int32, (B, B), 0)
    cols = lax.broadcasted_iota(jnp.int32, (B, B), 1)
    for r in range(NBR):
        for s in range(NBR):
            here = (pl.ds(r * B, B), pl.ds(s * B, B))
            if r < s:
                mine[r * NBR + s] = eta_ref[here]
            elif r > s:
                mine[r * NBR + s] = ham_ref[here]
            else:
                mine[r * NBR + s] = jnp.where(rows < cols, eta_ref[here], ham_ref[here])

    pl.semaphore_wait(barrier, 2 + has_up.astype(jnp.int32) + has_down.astype(jnp.int32))

    def remote(src, own, sem, target):
        return pltpu.make_async_remote_copy(
            src_ref=mine if own else all_ref.at[src],
            dst_ref=all_ref.at[src],
            send_sem=sem,
            recv_sem=recv.at[src],
            device_id=(group, target),
            device_id_type=MESH,
        )

    def arrived(src):
        remote(src, True, send_c.at[0], twin).wait_recv()

    def column_step(step, action):
        for way in (0, 1):
            if step == 0 and way == 1:
                continue
            lvl = level - step if way == 0 else level + step
            inside = lvl >= 0 if way == 0 else lvl < LEVELS

            @pl.when(inside)
            def _():
                action(step, way, lvl)

    def handle(step, way, lvl):
        src = chan_at(lvl, side, core)
        own = step == 0
        if not own:
            arrived(src)
        if own or way == 0:
            @pl.when(has_up)
            def _():
                remote(src, own, send_z.at[0, step], up).start()
        if own or way == 1:
            @pl.when(has_down)
            def _():
                remote(src, own, send_z.at[1, step], down).start()
        remote(src, own, send_x.at[way, step], across).start()
        remote(src, own, send_c.at[way * LEVELS + step], twin).start()

    def handle_across(step, way, lvl):
        src = chan_at(lvl, 1 - side, core)
        arrived(src)
        remote(src, False, send_c.at[2 * LEVELS + way * LEVELS + step], twin).start()

    column_step(0, handle)
    keep = pltpu.make_async_copy(mine, all_ref.at[me], local)
    keep.start()
    occ = occ_ref[...]
    for r in range(NBR):
        band = pl.ds(r * B, B)
        ladder_ref[band, :] = jnp.dot(
            eta_ref[band, :] * occ, ham_ref[...], preferred_element_type=jnp.float32
        ) - jnp.dot(ham_ref[band, :] * occ, eta_ref[...], preferred_element_type=jnp.float32)
    for step in range(1, LEVELS):
        column_step(step, handle)
        column_step(step - 1, handle_across)
    column_step(LEVELS - 1, handle_across)

    def finish(step, way, lvl):
        own = step == 0
        src = chan_at(lvl, side, core)
        if own or way == 0:
            @pl.when(has_up)
            def _():
                remote(src, own, send_z.at[0, step], up).wait_send()
        if own or way == 1:
            @pl.when(has_down)
            def _():
                remote(src, own, send_z.at[1, step], down).wait_send()
        remote(src, own, send_x.at[way, step], across).wait_send()
        remote(src, own, send_c.at[way * LEVELS + step], twin).wait_send()
        other = chan_at(lvl, 1 - side, core)
        remote(other, False, send_c.at[2 * LEVELS + way * LEVELS + step], twin).wait_send()

    def finish_twin(step, way, lvl):
        arrived(chan_at(lvl, side, 1 - core))
        arrived(chan_at(lvl, 1 - side, 1 - core))

    for step in range(LEVELS):
        column_step(step, finish_twin)
        column_step(step, finish)
    keep.wait()


def gather_packed(eta, ham, occ, chan_count):
    order = eta.shape[0]
    vmem = pl.BlockSpec(memory_space=pltpu.VMEM)
    return pl.pallas_call(
        gather_kernel,
        out_shape=(
            jax.ShapeDtypeStruct((chan_count, NBLK, B, B), jnp.bfloat16),
            jax.ShapeDtypeStruct((order, order), jnp.float32),
        ),
        in_specs=[vmem, vmem, vmem],
        out_specs=(pl.BlockSpec(memory_space=pl.ANY), vmem),
        scratch_shapes=[
            pltpu.VMEM((NBLK, B, B), jnp.bfloat16),
            pltpu.SemaphoreType.DMA((2, LEVELS)),
            pltpu.SemaphoreType.DMA((2, LEVELS)),
            pltpu.SemaphoreType.DMA((4 * LEVELS,)),
            pltpu.SemaphoreType.DMA((chan_count,)),
            pltpu.SemaphoreType.DMA,
        ],
        compiler_params=pltpu.CompilerParams(
            collective_id=0, has_side_effects=True, vmem_limit_bytes=LIMIT
        ),
    )(eta, ham, occ)


def recouple_kernel(refs, coef, picks, packed, occ, own_ref, twin_ref, eta_full, ham_full, mix_eta, mix_ham, z_tiles, sums):
    chan_count = packed.shape[0]
    local_count = occ.shape[0]
    rows = lax.broadcasted_iota(jnp.int32, (B, B), 0)
    cols = lax.broadcasted_iota(jnp.int32, (B, B), 1)

    @pl.loop(0, chan_count)
    def _(chan):
        base = chan * NBLK
        for r in range(NBR):
            both = packed[chan, r * NBR + r]
            flip = both.T
            zero = jnp.zeros_like(both)
            eta_full[base + r * NBR + r] = jnp.where(rows < cols, both, jnp.where(rows > cols, -flip, zero))
            ham_full[base + r * NBR + r] = jnp.where(rows >= cols, both, flip)
            for s in range(r + 1, NBR):
                high = packed[chan, r * NBR + s]
                low = packed[chan, s * NBR + r]
                eta_full[base + r * NBR + s] = high
                eta_full[base + s * NBR + r] = -(high.T)
                ham_full[base + s * NBR + r] = low
                ham_full[base + r * NBR + s] = low.T

    sums[...] = jnp.zeros_like(sums)
    half = B // 2

    @pl.loop(0, local_count)
    def _(q):
        @pl.loop(0, NBR)
        def _(r):
            for s in range(NBR):
                for part in range(2):
                    span = pl.ds(part * half, half)
                    total_eta = jnp.zeros((half, B), jnp.float32)
                    total_ham = jnp.zeros((half, B), jnp.float32)
                    for term in range(K):
                        at = (r * NBR + s) * K + term
                        which = refs[q, at]
                        weight = coef[q, at]
                        total_eta += eta_full[which, span, :].astype(jnp.float32) * weight
                        total_ham += ham_full[which, span, :].astype(jnp.float32) * weight
                    band = pl.ds(pl.multiple_of(r * B + part * half, half), half)
                    mix_eta[band, s * B : (s + 1) * B] = total_eta.astype(jnp.bfloat16)
                    mix_ham[band, s * B : (s + 1) * B] = total_ham.astype(jnp.bfloat16)

        scale = occ[q]

        @pl.loop(0, NBR)
        def _(r):
            band = pl.ds(pl.multiple_of(r * B, B), B)
            slab = jnp.dot(
                mix_eta[band, :] * scale, mix_ham[...], preferred_element_type=jnp.float32
            ) - jnp.dot(mix_ham[band, :] * scale, mix_eta[...], preferred_element_type=jnp.float32)
            for s in range(NBR):
                z_tiles[r * NBR + s] = slab[:, s * B : (s + 1) * B]

        @pl.loop(0, 2 * K)
        def _(slot):
            at = picks[q, slot]
            target = (slot // K) * NBLK + lax.rem(refs[q, at], NBLK)
            back = (z_tiles[at // K] * coef[q, at]).astype(jnp.bfloat16)
            sums[target] += back.astype(jnp.float32)

    for r in range(NBR):
        for s in range(NBR):
            here = (slice(r * B, (r + 1) * B), slice(s * B, (s + 1) * B))
            own_ref[here] = sums[r * NBR + s]
            twin_ref[here] = sums[NBLK + r * NBR + s]


def recouple(refs, coef, picks, packed, occ, order):
    chan_count = packed.shape[0]
    vmem = pl.BlockSpec(memory_space=pltpu.VMEM)
    smem = pl.BlockSpec(memory_space=pltpu.SMEM)
    return pl.pallas_call(
        recouple_kernel,
        out_shape=(jax.ShapeDtypeStruct((order, order), jnp.float32),) * 2,
        in_specs=[smem, smem, smem, vmem, vmem],
        out_specs=(vmem, vmem),
        scratch_shapes=[
            pltpu.VMEM((chan_count * NBLK, B, B), jnp.bfloat16),
            pltpu.VMEM((chan_count * NBLK, B, B), jnp.bfloat16),
            pltpu.VMEM((order, order), jnp.bfloat16),
            pltpu.VMEM((order, order), jnp.bfloat16),
            pltpu.VMEM((NBLK, B, B), jnp.float32),
            pltpu.VMEM((2 * NBLK, B, B), jnp.float32),
        ],
        compiler_params=pltpu.CompilerParams(vmem_limit_bytes=LIMIT),
    )(refs, coef, picks, packed, occ)


def gather_plan(eta, ham, pp_occ, ph_occ, ph_src, coef6j):
    chan_count = lax.axis_size("chan")
    order = eta.shape[0]
    me = lax.axis_index("chan")
    core = me % 2
    ladder_occ = (1 - pp_occ[0, 0] - pp_occ[0, 1]).astype(jnp.bfloat16)[None, :]
    meta = jnp.concatenate(
        [
            ph_src.reshape(1, TERMS).astype(jnp.float32),
            coef6j.reshape(1, TERMS),
            (ph_occ[0, 0] - ph_occ[0, 1]).astype(jnp.float32).reshape(order // TERMS, TERMS),
        ],
        axis=0,
    )
    tables = lax.all_gather(meta, "chan", axis=0, tiled=False)
    packed, ladder = gather_packed(eta, ham, ladder_occ, chan_count)
    mine = lax.dynamic_index_in_dim(
        tables.reshape(chan_count // 2, 2, -1, TERMS), core, axis=1, keepdims=False
    )
    refs = mine[:, 0].astype(jnp.int32)
    coef = mine[:, 1]
    occ = mine[:, 2:].reshape(-1, 1, order).astype(jnp.bfloat16)
    twin = me + 1 - 2 * core
    hits = refs[:, None, :] // NBLK == jnp.stack([me, twin])[None, :, None]
    rank = jnp.cumsum(hits.astype(jnp.int32), axis=-1) - 1
    slots = jnp.arange(K, dtype=jnp.int32)[None, None, :, None]
    chosen = hits[:, :, None, :] & (rank[:, :, None, :] == slots)
    picks = jnp.sum(
        jnp.where(chosen, jnp.arange(TERMS, dtype=jnp.int32), 0), axis=-1
    ).reshape(-1, 2 * K)
    own, other = recouple(refs, coef, picks, packed, occ, order)
    pairs = [(i, i + 1 - 2 * (i % 2)) for i in range(chan_count)]
    received = lax.ppermute(other, "chan", pairs)
    return ladder + own + received


def solution(mesh):
    chan_count = mesh.shape["chan"]
    plan = gather_plan if chan_count == LEVELS * 4 else exchange_plan
    return jax.shard_map(
        plan,
        mesh=mesh,
        in_specs=(
            P(("groups", "chan"), None),
            P(("groups", "chan"), None),
            P(("groups", "chan"), None, None),
            P(("groups", "chan"), None, None),
            P(("groups", "chan"), None, None),
            P(("groups", "chan"), None, None),
        ),
        out_specs=P(("groups", "chan"), None),
        check_vma=False,
    )
```

```python
import jax
import jax.numpy as jnp
from jax import lax
from jax.experimental import pallas as pl
from jax.experimental.pallas import tpu as pltpu
from jax.sharding import PartitionSpec as P

B = 128
NBR = 4
K = 8
NBLK = 16
TERMS = NBLK * K
MESH = pl.DeviceIdType.MESH
LIMIT = 48 * 1024 * 1024


def exchange_plan(eta, ham, pp_occ, ph_occ, ph_src, coef6j):
    chan_count = lax.axis_size("chan")
    chan_order = eta.shape[0]
    tile_size = B
    row_tiles = NBR
    tile_count = NBLK
    term_count = tile_count * K
    capacity = max(2, term_count // chan_count)

    def split_tiles(matrix):
        return (
            matrix.reshape(row_tiles, tile_size, row_tiles, tile_size)
            .transpose(0, 2, 1, 3)
            .reshape(tile_count, tile_size, tile_size)
        )

    def join_tiles(tiles):
        return (
            tiles.reshape(row_tiles, row_tiles, tile_size, tile_size)
            .transpose(0, 2, 1, 3)
            .reshape(chan_order, chan_order)
        )

    ref_list = ph_src.reshape(term_count)
    source = ref_list // tile_count
    within = ref_list % tile_count
    lane_ids = jnp.arange(chan_count, dtype=jnp.int32)
    hit_table = (source[:, None] == lane_ids[None, :]).astype(jnp.int32)
    slot_of = jnp.sum(jnp.cumsum(hit_table, axis=0) * hit_table, axis=1) - 1
    place_at = source * capacity + slot_of
    wanted = (
        jnp.full((chan_count * capacity,), -1, jnp.int32)
        .at[place_at]
        .set(within)
        .reshape(chan_count, capacity)
    )
    asked_for = lax.all_to_all(wanted, "chan", split_axis=0, concat_axis=0, tiled=True)
    weights = coef6j.reshape(tile_count, K)
    live = (asked_for >= 0)[:, :, None, None]
    safe_ids = jnp.maximum(asked_for, 0)

    def mix_terms(picked):
        shaped = picked.reshape(tile_count, K, tile_size, tile_size)
        total = jnp.zeros((tile_count, tile_size, tile_size), jnp.float32)
        for term in range(K):
            total = total + shaped[:, term].astype(jnp.float32) * weights[:, term][:, None, None]
        return join_tiles(total.astype(jnp.bfloat16))

    eta_tiles = split_tiles(eta)
    ham_tiles = split_tiles(ham)
    pair_blocks = jnp.stack([eta_tiles, ham_tiles], axis=1)
    outgoing = jnp.where(live[:, :, None], pair_blocks[safe_ids], jnp.zeros((), jnp.bfloat16))
    incoming = lax.all_to_all(outgoing, "chan", split_axis=0, concat_axis=0, tiled=True)
    picked = incoming.reshape(chan_count * capacity, 2, tile_size, tile_size)[place_at]
    ph_eta = mix_terms(picked[:, 0])
    ph_ham = mix_terms(picked[:, 1])
    occ_ph = (ph_occ[0, 0] - ph_occ[0, 1]).astype(jnp.bfloat16)
    z_matrix = jnp.dot(
        ph_eta * occ_ph[None, :], ph_ham, preferred_element_type=jnp.float32
    ) - jnp.dot(ph_ham * occ_ph[None, :], ph_eta, preferred_element_type=jnp.float32)
    back_terms = (
        (split_tiles(z_matrix)[:, None] * weights[:, :, None, None])
        .astype(jnp.bfloat16)
        .reshape(term_count, tile_size, tile_size)
    )
    outgoing_back = (
        jnp.zeros((chan_count * capacity, tile_size, tile_size), jnp.bfloat16)
        .at[place_at]
        .set(back_terms)
        .reshape(chan_count, capacity, tile_size, tile_size)
    )
    returned = lax.all_to_all(outgoing_back, "chan", split_axis=0, concat_axis=0, tiled=True)
    tile_ids = jnp.arange(tile_count, dtype=jnp.int32)
    selector = (asked_for.reshape(chan_count * capacity)[None, :] == tile_ids[:, None]).astype(
        jnp.bfloat16
    )
    ph_term = jnp.dot(
        selector,
        returned.reshape(chan_count * capacity, tile_size * tile_size),
        preferred_element_type=jnp.float32,
    ).reshape(tile_count, tile_size, tile_size)
    occ_pp = (1 - pp_occ[0, 0] - pp_occ[0, 1]).astype(jnp.bfloat16)
    ladder = jnp.dot(eta * occ_pp[None, :], ham, preferred_element_type=jnp.float32) - jnp.dot(
        ham * occ_pp[None, :], eta, preferred_element_type=jnp.float32
    )
    return ladder + join_tiles(ph_term)


LEVELS = 4
HALVES = 2
PER_HALF = NBLK // HALVES
TABLE = 16
CHUNK = PER_HALF * B + TABLE


def flow_kernel(
    eta_ref, ham_ref, pp_occ_ref, ph_occ_ref, src_ref, coef_ref, out_ref,
    packed, eta_full, ham_full, left, right, z_tiles, outbound, inbound,
    src_table, coef_table, pick_table, gain_table, refs, weights, picks, gains,
    send_z, send_x, send_c, recv, local, send_sum, recv_sum,
):
    group = lax.axis_index("groups")
    me = lax.axis_index("chan")
    level = me // 4
    side = (me // 2) % 2
    core = me % 2
    chan_count = packed.shape[0]
    local_count = chan_count // 2

    def chan_at(lvl, sd, cr):
        return (lvl * 2 + sd) * 2 + cr

    up = chan_at(level + 1, side, core)
    down = chan_at(level - 1, side, core)
    across = chan_at(level, 1 - side, core)
    twin = chan_at(level, side, 1 - core)
    has_up = level < LEVELS - 1
    has_down = level > 0
    mate = level + 1 - 2 * (level % 2)

    barrier = pltpu.get_barrier_semaphore()

    def greet(target):
        pl.semaphore_signal(barrier, inc=1, device_id=(group, target), device_id_type=MESH)

    greet(across)
    greet(twin)

    @pl.when(has_up)
    def _():
        greet(up)

    @pl.when(has_down)
    def _():
        greet(down)

    rows = lax.broadcasted_iota(jnp.int32, (B, B), 0)
    cols = lax.broadcasted_iota(jnp.int32, (B, B), 1)

    def tile_rows(block):
        return block // PER_HALF, pl.ds((block % PER_HALF) * B, B)

    for r in range(NBR):
        for s in range(NBR):
            here = (pl.ds(r * B, B), pl.ds(s * B, B))
            if r < s:
                tile = eta_ref[here]
            elif r > s:
                tile = ham_ref[here]
            else:
                tile = jnp.where(rows < cols, eta_ref[here], ham_ref[here])
            half, band = tile_rows(r * NBR + s)
            packed[me, half, band, :] = tile
    coef = coef_ref[...]
    first = coef.astype(jnp.bfloat16)
    rest = coef - first.astype(jnp.float32)
    second = rest.astype(jnp.bfloat16)
    third = (rest - second.astype(jnp.float32)).astype(jnp.bfloat16)
    table = jnp.concatenate(
        [
            src_ref[...].astype(jnp.float32),
            first.astype(jnp.float32),
            second.astype(jnp.float32),
            third.astype(jnp.float32),
            ph_occ_ref[...].astype(jnp.float32),
            jnp.zeros((TABLE - 8, B), jnp.float32),
        ],
        axis=0,
    )
    for half in range(HALVES):
        packed[me, half, PER_HALF * B :, :] = table.astype(jnp.bfloat16)

    pl.semaphore_wait(barrier, 2 + has_up.astype(jnp.int32) + has_down.astype(jnp.int32))

    def remote(src, half, sem, target):
        return pltpu.make_async_remote_copy(
            src_ref=packed.at[src, half],
            dst_ref=packed.at[src, half],
            send_sem=sem,
            recv_sem=recv.at[src, half],
            device_id=(group, target),
            device_id_type=MESH,
        )

    def arrived(src, half):
        remote(src, half, send_c.at[0, 0, 0, 0], twin).wait_recv()

    def moves(step, way, lvl, half, act):
        src = chan_at(lvl, side, core)
        if step == 0 or way == 0:
            @pl.when(has_up)
            def _():
                act(remote(src, half, send_z.at[0, step, half], up))
        if step == 0 or way == 1:
            @pl.when(has_down)
            def _():
                act(remote(src, half, send_z.at[1, step, half], down))
        if half == 1 and step == 1:
            @pl.when(lvl != mate)
            def _():
                act(remote(src, half, send_x.at[way, step, half], across))
        else:
            act(remote(src, half, send_x.at[way, step, half], across))
        act(remote(src, half, send_c.at[0, way, step, half], twin))

    def across_moves(step, way, lvl, half, act):
        src = chan_at(lvl, 1 - side, core)
        act(remote(src, half, send_c.at[1, way, step, half], twin))
        if half == 1 and step == 0:
            act(remote(src, half, send_z.at[0, LEVELS, half], chan_at(mate, side, core)))

    def each_way(step, action):
        for way in range(2 if step else 1):
            lvl = level - step if way == 0 else level + step
            inside = lvl >= 0 if way == 0 else lvl < LEVELS

            @pl.when(inside)
            def _():
                action(way, lvl)

    def column(step):
        for half in range(HALVES):
            def action(way, lvl):
                if step:
                    arrived(chan_at(lvl, side, core), half)
                moves(step, way, lvl, half, lambda copy: copy.start())

            each_way(step, action)

    def crossing(step):
        for half in range(HALVES):
            def action(way, lvl):
                arrived(chan_at(lvl, 1 - side, core), half)
                across_moves(step, way, lvl, half, lambda copy: copy.start())

            each_way(step, action)

    def expand(src):
        base = src * NBLK
        for r in range(NBR):
            for s in range(NBR):
                half, band = tile_rows(r * NBR + s)
                tile = packed[src, half, band, :]
                flip = tile.T
                if r < s:
                    eta_full[base + r * NBR + s] = tile
                    eta_full[base + s * NBR + r] = -flip
                elif r > s:
                    ham_full[base + r * NBR + s] = tile
                    ham_full[base + s * NBR + r] = flip
                else:
                    zero = jnp.zeros_like(tile)
                    eta_full[base + r * NBR + s] = jnp.where(
                        rows < cols, tile, jnp.where(rows > cols, -flip, zero)
                    )
                    ham_full[base + r * NBR + s] = jnp.where(rows >= cols, tile, flip)

    def expand_all(step, members):
        ways = 2 if step else 1

        @pl.loop(0, ways * len(members))
        def _(turn):
            way = turn % ways
            lvl = level + (2 * way - 1) * step

            @pl.when((lvl >= 0) & (lvl < LEVELS))
            def _():
                place = members[0] if len(members) == 1 else turn // ways
                if len(members) == 1:
                    sd, cr = place
                    src = chan_at(lvl, sd, cr)
                else:
                    src = chan_at(lvl, place, 1 - core)
                    for half in range(HALVES):
                        arrived(src, half)
                expand(src)

    def expand_twin(step):
        expand_all(step, (0, 1))

    column(0)
    occ = pp_occ_ref[...]
    for r in range(NBR):
        band = pl.ds(r * B, B)
        out_ref[band, :] = jnp.dot(
            eta_ref[band, :] * occ, ham_ref[...], preferred_element_type=jnp.float32
        ) - jnp.dot(ham_ref[band, :] * occ, eta_ref[...], preferred_element_type=jnp.float32)
    expand_all(0, ((side, core),))
    for step in range(1, LEVELS):
        column(step)
        crossing(step - 1)
        expand_all(step, ((side, core),))
        expand_all(step - 1, ((1 - side, core),))
        if step >= 2:
            expand_twin(step - 2)
    crossing(LEVELS - 1)
    expand_twin(LEVELS - 2)
    expand_all(LEVELS - 1, ((1 - side, core),))
    expand_twin(LEVELS - 1)

    for q in range(local_count):
        table = packed[2 * q + core, 0, PER_HALF * B :, :].astype(jnp.float32)
        src_table[q : q + 1, :] = jnp.clip(
            table[0:1, :].astype(jnp.int32), 0, chan_count * NBLK - 1
        )
        coef_table[q : q + 1, :] = table[1:2, :] + (table[2:3, :] + table[3:4, :])
    loads = [
        pltpu.make_async_copy(src_table, refs, local.at[0]),
        pltpu.make_async_copy(coef_table, weights, local.at[1]),
    ]
    for load in loads:
        load.start()
    named = src_table[...]
    factor = coef_table[...]
    lanes = lax.broadcasted_iota(jnp.int32, named.shape, 1)
    found = jnp.zeros(named.shape, jnp.int32)
    gain = jnp.zeros(named.shape, jnp.float32)
    for place in range(2 * NBLK):
        owner = me if place < NBLK else twin
        hit = named == owner * NBLK + place % NBLK
        tile = jnp.max(jnp.where(hit, lanes // K, 0), axis=1, keepdims=True)
        scale = jnp.sum(jnp.where(hit, factor, 0.0), axis=1, keepdims=True)
        found = jnp.where(lanes == place, tile, found)
        gain = jnp.where(lanes == place, scale, gain)
    pick_table[...] = found
    gain_table[...] = gain
    more = [
        pltpu.make_async_copy(pick_table, picks, local.at[2]),
        pltpu.make_async_copy(gain_table, gains, local.at[3]),
    ]
    for load in more:
        load.start()
    for load in loads:
        load.wait()

    part_rows = B // 2
    order = NBR * B

    @pl.loop(0, local_count)
    def _(q):
        @pl.loop(0, NBR)
        def _(r):
            for s in range(NBR):
                scale = packed[2 * q + core, 0, PER_HALF * B :, :][4 + s : 5 + s, :]
                for part in range(2):
                    span = pl.ds(part * part_rows, part_rows)
                    total_eta = jnp.zeros((part_rows, B), jnp.float32)
                    total_ham = jnp.zeros((part_rows, B), jnp.float32)
                    for term in range(K):
                        at = (r * NBR + s) * K + term
                        which = refs[q, at]
                        weight = weights[q, at]
                        total_eta += eta_full[which, span, :].astype(jnp.float32) * weight
                        total_ham += ham_full[which, span, :].astype(jnp.float32) * weight
                    start = pl.multiple_of(r * B + part * part_rows, part_rows)
                    lane = slice(s * B, (s + 1) * B)
                    beyond = slice(order + s * B, order + (s + 1) * B)
                    mixed_eta = total_eta.astype(jnp.bfloat16)
                    mixed_ham = total_ham.astype(jnp.bfloat16)
                    left[pl.ds(start, part_rows), lane] = mixed_eta * scale
                    left[pl.ds(start, part_rows), beyond] = -(mixed_ham * scale)
                    right[pl.ds(start, part_rows), lane] = mixed_ham
                    right[pl.ds(order + start, part_rows), lane] = mixed_eta

        @pl.loop(0, NBR)
        def _(r):
            band = pl.ds(pl.multiple_of(r * B, B), B)
            slab = jnp.dot(left[band, :], right[...], preferred_element_type=jnp.float32)
            for s in range(NBR):
                z_tiles[q * NBLK + r * NBR + s] = slab[:, s * B : (s + 1) * B]

    for load in more:
        load.wait()

    def sum_back(first, target, keep):
        @pl.loop(0, NBR)
        def _(r):
            for s in range(NBR):
                for part in range(2):
                    span = pl.ds(part * part_rows, part_rows)
                    total = jnp.zeros((part_rows, B), jnp.float32)
                    for q in range(local_count):
                        at = first + r * NBR + s
                        tile = z_tiles[q * NBLK + picks[q, at], span, :]
                        total += (tile * gains[q, at]).astype(jnp.bfloat16).astype(jnp.float32)
                    start = pl.multiple_of(r * B + part * part_rows, part_rows)
                    here = (pl.ds(start, part_rows), slice(s * B, (s + 1) * B))
                    target[here] = target[here] + total if keep else total

    sum_back(NBLK, outbound, False)
    swap = pltpu.make_async_remote_copy(
        src_ref=outbound,
        dst_ref=inbound,
        send_sem=send_sum,
        recv_sem=recv_sum,
        device_id=(group, twin),
        device_id_type=MESH,
    )
    swap.start()
    sum_back(0, out_ref, True)

    for step in range(LEVELS):
        for half in range(HALVES):
            each_way(step, lambda way, lvl: moves(step, way, lvl, half, lambda copy: copy.wait_send()))
            each_way(
                step, lambda way, lvl: across_moves(step, way, lvl, half, lambda copy: copy.wait_send())
            )
    swap.wait()
    out_ref[...] += inbound[...]


def gather_plan(eta, ham, pp_occ, ph_occ, ph_src, coef6j):
    chan_count = lax.axis_size("chan")
    order = eta.shape[0]
    pp_scale = (1 - pp_occ[0, 0] - pp_occ[0, 1]).astype(jnp.bfloat16)[None, :]
    ph_scale = (ph_occ[0, 0] - ph_occ[0, 1]).reshape(NBR, B)
    vmem = pl.BlockSpec(memory_space=pltpu.VMEM)
    blocks = chan_count * NBLK
    mine = chan_count // 2
    return pl.pallas_call(
        flow_kernel,
        out_shape=jax.ShapeDtypeStruct((order, order), jnp.float32),
        in_specs=[vmem] * 6,
        out_specs=vmem,
        scratch_shapes=[
            pltpu.VMEM((chan_count, HALVES, CHUNK, B), jnp.bfloat16),
            pltpu.VMEM((blocks, B, B), jnp.bfloat16),
            pltpu.VMEM((blocks, B, B), jnp.bfloat16),
            pltpu.VMEM((order, 2 * order), jnp.bfloat16),
            pltpu.VMEM((2 * order, order), jnp.bfloat16),
            pltpu.VMEM((mine * NBLK, B, B), jnp.float32),
            pltpu.VMEM((order, order), jnp.float32),
            pltpu.VMEM((order, order), jnp.float32),
            pltpu.VMEM((mine, TERMS), jnp.int32),
            pltpu.VMEM((mine, TERMS), jnp.float32),
            pltpu.VMEM((mine, TERMS), jnp.int32),
            pltpu.VMEM((mine, TERMS), jnp.float32),
            pltpu.SMEM((mine, TERMS), jnp.int32),
            pltpu.SMEM((mine, TERMS), jnp.float32),
            pltpu.SMEM((mine, TERMS), jnp.int32),
            pltpu.SMEM((mine, TERMS), jnp.float32),
            pltpu.SemaphoreType.DMA((2, LEVELS + 1, HALVES)),
            pltpu.SemaphoreType.DMA((2, LEVELS, HALVES)),
            pltpu.SemaphoreType.DMA((2, 2, LEVELS, HALVES)),
            pltpu.SemaphoreType.DMA((chan_count, HALVES)),
            pltpu.SemaphoreType.DMA((4,)),
            pltpu.SemaphoreType.DMA,
            pltpu.SemaphoreType.DMA,
        ],
        compiler_params=pltpu.CompilerParams(
            collective_id=0, has_side_effects=True, vmem_limit_bytes=LIMIT
        ),
    )(eta, ham, pp_scale, ph_scale, ph_src.reshape(1, TERMS), coef6j.reshape(1, TERMS))


def solution(mesh):
    chan_count = mesh.shape["chan"]
    plan = gather_plan if chan_count == LEVELS * 4 else exchange_plan
    return jax.shard_map(
        plan,
        mesh=mesh,
        in_specs=(
            P(("groups", "chan"), None),
            P(("groups", "chan"), None),
            P(("groups", "chan"), None, None),
            P(("groups", "chan"), None, None),
            P(("groups", "chan"), None, None),
            P(("groups", "chan"), None, None),
        ),
        out_specs=P(("groups", "chan"), None),
        check_vma=False,
    )
```

```python
import jax
import jax.numpy as jnp
from jax import lax
from jax.experimental import pallas as pl
from jax.experimental.pallas import tpu as pltpu
from jax.sharding import PartitionSpec as P

B = 128
NBR = 4
K = 8
NBLK = 16
TERMS = NBLK * K
MESH = pl.DeviceIdType.MESH
LIMIT = 60 * 1024 * 1024


def exchange_plan(eta, ham, pp_occ, ph_occ, ph_src, coef6j):
    chan_count = lax.axis_size("chan")
    chan_order = eta.shape[0]
    tile_size = B
    row_tiles = NBR
    tile_count = NBLK
    term_count = tile_count * K
    capacity = max(2, term_count // chan_count)

    def split_tiles(matrix):
        return (
            matrix.reshape(row_tiles, tile_size, row_tiles, tile_size)
            .transpose(0, 2, 1, 3)
            .reshape(tile_count, tile_size, tile_size)
        )

    def join_tiles(tiles):
        return (
            tiles.reshape(row_tiles, row_tiles, tile_size, tile_size)
            .transpose(0, 2, 1, 3)
            .reshape(chan_order, chan_order)
        )

    ref_list = ph_src.reshape(term_count)
    source = ref_list // tile_count
    within = ref_list % tile_count
    lane_ids = jnp.arange(chan_count, dtype=jnp.int32)
    hit_table = (source[:, None] == lane_ids[None, :]).astype(jnp.int32)
    slot_of = jnp.sum(jnp.cumsum(hit_table, axis=0) * hit_table, axis=1) - 1
    place_at = source * capacity + slot_of
    wanted = (
        jnp.full((chan_count * capacity,), -1, jnp.int32)
        .at[place_at]
        .set(within)
        .reshape(chan_count, capacity)
    )
    asked_for = lax.all_to_all(wanted, "chan", split_axis=0, concat_axis=0, tiled=True)
    weights = coef6j.reshape(tile_count, K)
    live = (asked_for >= 0)[:, :, None, None]
    safe_ids = jnp.maximum(asked_for, 0)

    def mix_terms(picked):
        shaped = picked.reshape(tile_count, K, tile_size, tile_size)
        total = jnp.zeros((tile_count, tile_size, tile_size), jnp.float32)
        for term in range(K):
            total = total + shaped[:, term].astype(jnp.float32) * weights[:, term][:, None, None]
        return join_tiles(total.astype(jnp.bfloat16))

    eta_tiles = split_tiles(eta)
    ham_tiles = split_tiles(ham)
    pair_blocks = jnp.stack([eta_tiles, ham_tiles], axis=1)
    outgoing = jnp.where(live[:, :, None], pair_blocks[safe_ids], jnp.zeros((), jnp.bfloat16))
    incoming = lax.all_to_all(outgoing, "chan", split_axis=0, concat_axis=0, tiled=True)
    picked = incoming.reshape(chan_count * capacity, 2, tile_size, tile_size)[place_at]
    ph_eta = mix_terms(picked[:, 0])
    ph_ham = mix_terms(picked[:, 1])
    occ_ph = (ph_occ[0, 0] - ph_occ[0, 1]).astype(jnp.bfloat16)
    z_matrix = jnp.dot(
        ph_eta * occ_ph[None, :], ph_ham, preferred_element_type=jnp.float32
    ) - jnp.dot(ph_ham * occ_ph[None, :], ph_eta, preferred_element_type=jnp.float32)
    back_terms = (
        (split_tiles(z_matrix)[:, None] * weights[:, :, None, None])
        .astype(jnp.bfloat16)
        .reshape(term_count, tile_size, tile_size)
    )
    outgoing_back = (
        jnp.zeros((chan_count * capacity, tile_size, tile_size), jnp.bfloat16)
        .at[place_at]
        .set(back_terms)
        .reshape(chan_count, capacity, tile_size, tile_size)
    )
    returned = lax.all_to_all(outgoing_back, "chan", split_axis=0, concat_axis=0, tiled=True)
    tile_ids = jnp.arange(tile_count, dtype=jnp.int32)
    selector = (asked_for.reshape(chan_count * capacity)[None, :] == tile_ids[:, None]).astype(
        jnp.bfloat16
    )
    ph_term = jnp.dot(
        selector,
        returned.reshape(chan_count * capacity, tile_size * tile_size),
        preferred_element_type=jnp.float32,
    ).reshape(tile_count, tile_size, tile_size)
    occ_pp = (1 - pp_occ[0, 0] - pp_occ[0, 1]).astype(jnp.bfloat16)
    ladder = jnp.dot(eta * occ_pp[None, :], ham, preferred_element_type=jnp.float32) - jnp.dot(
        ham * occ_pp[None, :], eta, preferred_element_type=jnp.float32
    )
    return ladder + join_tiles(ph_term)


LEVELS = 4
HALVES = 2
PER_HALF = NBLK // HALVES
TABLE = 16
CHUNK = PER_HALF * B + TABLE


def flat(values):
    return jnp.concatenate([values[k : k + 1, :] for k in range(K)], axis=1)


def flow_kernel(
    eta_hbm, ham_hbm, pp_occ_hbm, ph_occ_hbm, src_hbm, coef_hbm, out_ref,
    eta_ref, ham_ref, pp_occ_ref, ph_occ_ref, src_ref, coef_ref, packed, eta_full, ham_full, left, right, z_tiles, outbound, inbound,
    src_table, coef_table, pick_table, gain_table, refs, weights, picks, gains,
    send_z, send_x, send_c, recv, local, fetch, send_sum, recv_sum,
):
    group = lax.axis_index("groups")
    me = lax.axis_index("chan")
    level = me // 4
    side = (me // 2) % 2
    core = me % 2
    chan_count = packed.shape[0]
    local_count = chan_count // 2

    def chan_at(lvl, sd, cr):
        return (lvl * 2 + sd) * 2 + cr

    up = chan_at(level + 1, side, core)
    down = chan_at(level - 1, side, core)
    across = chan_at(level, 1 - side, core)
    twin = chan_at(level, side, 1 - core)
    has_up = level < LEVELS - 1
    has_down = level > 0
    mate = level + 1 - 2 * (level % 2)

    barrier = pltpu.get_barrier_semaphore()

    def greet(target):
        pl.semaphore_signal(barrier, inc=1, device_id=(group, target), device_id_type=MESH)

    greet(across)
    greet(twin)

    @pl.when(has_up)
    def _():
        greet(up)

    @pl.when(has_down)
    def _():
        greet(down)

    inputs = (eta_hbm, ham_hbm, src_hbm, coef_hbm, ph_occ_hbm, pp_occ_hbm)
    places = (eta_ref, ham_ref, src_ref, coef_ref, ph_occ_ref, pp_occ_ref)
    fetches = [
        pltpu.make_async_copy(there, here, fetch.at[i])
        for i, (there, here) in enumerate(zip(inputs, places))
    ]
    for copy in fetches:
        copy.start()
    rows = lax.broadcasted_iota(jnp.int32, (B, B), 0)
    cols = lax.broadcasted_iota(jnp.int32, (B, B), 1)

    def tile_rows(block):
        return block // PER_HALF, pl.ds((block % PER_HALF) * B, B)

    for copy in fetches:
        copy.wait()
    for r in range(NBR):
        for s in range(NBR):
            here = (pl.ds(r * B, B), pl.ds(s * B, B))
            if r < s:
                tile = eta_ref[here]
            elif r > s:
                tile = ham_ref[here]
            else:
                tile = jnp.where(rows < cols, eta_ref[here], ham_ref[here])
            half, band = tile_rows(r * NBR + s)
            packed[me, half, band, :] = tile
    coef = flat(coef_ref[...])
    first = coef.astype(jnp.bfloat16)
    rest = coef - first.astype(jnp.float32)
    second = rest.astype(jnp.bfloat16)
    third = (rest - second.astype(jnp.float32)).astype(jnp.bfloat16)
    occ_row = (ph_occ_ref[0:1, :] - ph_occ_ref[1:2, :]).astype(jnp.float32)
    table = jnp.concatenate(
        [
            flat(src_ref[...].astype(jnp.float32)),
            first.astype(jnp.float32),
            second.astype(jnp.float32),
            third.astype(jnp.float32),
            *[occ_row[:, s * B : (s + 1) * B] for s in range(NBR)],
            jnp.zeros((TABLE - 8, B), jnp.float32),
        ],
        axis=0,
    )
    for half in range(HALVES):
        packed[me, half, PER_HALF * B :, :] = table.astype(jnp.bfloat16)

    pl.semaphore_wait(barrier, 2 + has_up.astype(jnp.int32) + has_down.astype(jnp.int32))

    def remote(src, half, sem, target):
        return pltpu.make_async_remote_copy(
            src_ref=packed.at[src, half],
            dst_ref=packed.at[src, half],
            send_sem=sem,
            recv_sem=recv.at[src, half],
            device_id=(group, target),
            device_id_type=MESH,
        )

    def arrived(src, half):
        remote(src, half, send_c.at[0, 0, 0, 0], twin).wait_recv()

    def moves(step, way, lvl, half, act):
        src = chan_at(lvl, side, core)
        if step == 0 or way == 0:
            @pl.when(has_up)
            def _():
                act(remote(src, half, send_z.at[0, step, half], up))
        if step == 0 or way == 1:
            @pl.when(has_down)
            def _():
                act(remote(src, half, send_z.at[1, step, half], down))
        if half >= HALVES // 2 and step == 1:
            @pl.when(lvl != mate)
            def _():
                act(remote(src, half, send_x.at[way, step, half], across))
        else:
            act(remote(src, half, send_x.at[way, step, half], across))
        act(remote(src, half, send_c.at[0, way, step, half], twin))

    def across_moves(step, way, lvl, half, act):
        src = chan_at(lvl, 1 - side, core)
        act(remote(src, half, send_c.at[1, way, step, half], twin))
        if half >= HALVES // 2 and step == 0:
            act(remote(src, half, send_z.at[0, LEVELS, half], chan_at(mate, side, core)))

    def each_way(step, action):
        for way in range(2 if step else 1):
            lvl = level - step if way == 0 else level + step
            inside = lvl >= 0 if way == 0 else lvl < LEVELS

            @pl.when(inside)
            def _():
                action(way, lvl)

    def column(step):
        for half in range(HALVES):
            def action(way, lvl):
                if step:
                    arrived(chan_at(lvl, side, core), half)
                moves(step, way, lvl, half, lambda copy: copy.start())

            each_way(step, action)

    def crossing(step, begin=0, end=HALVES):
        for half in range(begin, end):
            def action(way, lvl):
                arrived(chan_at(lvl, 1 - side, core), half)
                across_moves(step, way, lvl, half, lambda copy: copy.start())

            each_way(step, action)

    def expand(src):
        base = src * NBLK
        for r in range(NBR):
            for s in range(NBR):
                half, band = tile_rows(r * NBR + s)
                tile = packed[src, half, band, :].astype(jnp.float32)
                flip = tile.T
                if r < s:
                    eta_full[base + r * NBR + s] = tile
                    eta_full[base + s * NBR + r] = -flip
                elif r > s:
                    ham_full[base + r * NBR + s] = tile
                    ham_full[base + s * NBR + r] = flip
                else:
                    zero = jnp.zeros_like(tile)
                    eta_full[base + r * NBR + s] = jnp.where(
                        rows < cols, tile, jnp.where(rows > cols, -flip, zero)
                    )
                    ham_full[base + r * NBR + s] = jnp.where(rows >= cols, tile, flip)

    def expand_all(step, members):
        ways = 2 if step else 1

        @pl.loop(0, ways * len(members))
        def _(turn):
            way = turn % ways
            lvl = level + (2 * way - 1) * step

            @pl.when((lvl >= 0) & (lvl < LEVELS))
            def _():
                place = members[0] if len(members) == 1 else turn // ways
                if len(members) == 1:
                    sd, cr = place
                    src = chan_at(lvl, sd, cr)
                else:
                    src = chan_at(lvl, place, 1 - core)
                    for half in range(HALVES):
                        arrived(src, half)
                expand(src)

    def expand_twin(step):
        expand_all(step, (0, 1))

    column(0)
    occ = (1 - pp_occ_ref[0:1, :] - pp_occ_ref[1:2, :]).astype(jnp.bfloat16)
    for r in range(NBR):
        band = pl.ds(r * B, B)
        out_ref[band, :] = jnp.dot(
            eta_ref[band, :] * occ, ham_ref[...], preferred_element_type=jnp.float32
        ) - jnp.dot(ham_ref[band, :] * occ, eta_ref[...], preferred_element_type=jnp.float32)
    expand_all(0, ((side, core),))
    for step in range(1, LEVELS):
        column(step)
        crossing(step - 1)
        expand_all(step, ((side, core),))
        expand_all(step - 1, ((1 - side, core),))
        if step >= 2:
            expand_twin(step - 2)
    crossing(LEVELS - 1, 0, 1)
    for q in range(local_count):
        table = packed[2 * q + core, 0, PER_HALF * B :, :].astype(jnp.float32)
        src_table[q : q + 1, :] = jnp.clip(
            table[0:1, :].astype(jnp.int32), 0, chan_count * NBLK - 1
        )
        coef_table[q : q + 1, :] = table[1:2, :] + (table[2:3, :] + table[3:4, :])
    loads = [
        pltpu.make_async_copy(src_table, refs, local.at[0]),
        pltpu.make_async_copy(coef_table, weights, local.at[1]),
    ]
    for load in loads:
        load.start()
    named = src_table[...]
    factor = coef_table[...]
    lanes = lax.broadcasted_iota(jnp.int32, named.shape, 1)
    found = jnp.zeros(named.shape, jnp.int32)
    gain = jnp.zeros(named.shape, jnp.float32)
    for place in range(2 * NBLK):
        owner = me if place < NBLK else twin
        hit = named == owner * NBLK + place % NBLK
        tile = jnp.max(jnp.where(hit, lanes % NBLK, 0), axis=1, keepdims=True)
        scale = jnp.sum(jnp.where(hit, factor, 0.0), axis=1, keepdims=True)
        found = jnp.where(lanes == place, tile, found)
        gain = jnp.where(lanes == place, scale, gain)
    pick_table[...] = found
    gain_table[...] = gain
    more = [
        pltpu.make_async_copy(pick_table, picks, local.at[2]),
        pltpu.make_async_copy(gain_table, gains, local.at[3]),
    ]
    for load in more:
        load.start()
    crossing(LEVELS - 1, 1, HALVES)
    expand_twin(LEVELS - 2)
    expand_all(LEVELS - 1, ((1 - side, core),))
    expand_twin(LEVELS - 1)

    for load in loads:
        load.wait()

    part_rows = B // 2
    order = NBR * B

    @pl.loop(0, local_count)
    def _(q):
        @pl.loop(0, NBR)
        def _(r):
            for s in range(NBR):
                scale = packed[2 * q + core, 0, PER_HALF * B :, :][4 + s : 5 + s, :]
                for part in range(2):
                    span = pl.ds(part * part_rows, part_rows)
                    total_eta = jnp.zeros((part_rows, B), jnp.float32)
                    total_ham = jnp.zeros((part_rows, B), jnp.float32)
                    for term in range(K):
                        at = term * NBLK + r * NBR + s
                        which = refs[q, at]
                        weight = weights[q, at]
                        total_eta += eta_full[which, span, :] * weight
                        total_ham += ham_full[which, span, :] * weight
                    start = pl.multiple_of(r * B + part * part_rows, part_rows)
                    lane = slice(s * B, (s + 1) * B)
                    beyond = slice(order + s * B, order + (s + 1) * B)
                    mixed_eta = total_eta.astype(jnp.bfloat16)
                    mixed_ham = total_ham.astype(jnp.bfloat16)
                    left[pl.ds(start, part_rows), lane] = mixed_eta * scale
                    left[pl.ds(start, part_rows), beyond] = -(mixed_ham * scale)
                    right[pl.ds(start, part_rows), lane] = mixed_ham
                    right[pl.ds(order + start, part_rows), lane] = mixed_eta

        for pair in range(NBR // 2):
            lane = slice(2 * pair * B, 2 * (pair + 1) * B)
            slab = jnp.dot(left[...], right[:, lane], preferred_element_type=jnp.float32)
            for r in range(NBR):
                for s in range(2):
                    z_tiles[q * NBLK + r * NBR + 2 * pair + s] = slab[
                        r * B : (r + 1) * B, s * B : (s + 1) * B
                    ]

    for load in more:
        load.wait()

    def sum_back(first, target, r, keep):
        for s in range(NBR):
            for part in range(2):
                span = pl.ds(part * part_rows, part_rows)
                total = jnp.zeros((part_rows, B), jnp.float32)
                for q in range(local_count):
                    at = first + r * NBR + s
                    tile = z_tiles[q * NBLK + picks[q, at], span, :]
                    total += tile * gains[q, at]
                here = (
                    slice(r * B + part * part_rows, r * B + (part + 1) * part_rows),
                    slice(s * B, (s + 1) * B),
                )
                target[here] = target[here] + total if keep else total

    swaps = []
    for r in range(NBR):
        sum_back(NBLK, outbound, r, False)
        swap = pltpu.make_async_remote_copy(
            src_ref=outbound.at[pl.ds(r * B, B)],
            dst_ref=inbound.at[pl.ds(r * B, B)],
            send_sem=send_sum.at[r],
            recv_sem=recv_sum.at[r],
            device_id=(group, twin),
            device_id_type=MESH,
        )
        swap.start()
        swaps.append(swap)
    for r in range(NBR):
        sum_back(0, out_ref, r, True)

    for step in range(LEVELS):
        for half in range(HALVES):
            each_way(step, lambda way, lvl: moves(step, way, lvl, half, lambda copy: copy.wait_send()))
            each_way(
                step, lambda way, lvl: across_moves(step, way, lvl, half, lambda copy: copy.wait_send())
            )
    for r, swap in enumerate(swaps):
        swap.wait()
        band = slice(r * B, (r + 1) * B)
        out_ref[band, :] += inbound[band, :]


def gather_plan(eta, ham, pp_occ, ph_occ, ph_src, coef6j):
    chan_count = lax.axis_size("chan")
    order = eta.shape[0]
    vmem = pl.BlockSpec(memory_space=pltpu.VMEM)
    blocks = chan_count * NBLK
    mine = chan_count // 2
    return pl.pallas_call(
        flow_kernel,
        out_shape=jax.ShapeDtypeStruct((order, order), jnp.float32),
        in_specs=[pl.BlockSpec(memory_space=pl.ANY)] * 6,
        out_specs=vmem,
        scratch_shapes=[
            pltpu.VMEM((order, order), jnp.bfloat16),
            pltpu.VMEM((order, order), jnp.bfloat16),
            pltpu.VMEM((2, order), jnp.int32),
            pltpu.VMEM((2, order), jnp.int32),
            pltpu.VMEM((K, NBLK), jnp.int32),
            pltpu.VMEM((K, NBLK), jnp.float32),
            pltpu.VMEM((chan_count, HALVES, CHUNK, B), jnp.bfloat16),
            pltpu.VMEM((blocks, B, B), jnp.float32),
            pltpu.VMEM((blocks, B, B), jnp.float32),
            pltpu.VMEM((order, 2 * order), jnp.bfloat16),
            pltpu.VMEM((2 * order, order), jnp.bfloat16),
            pltpu.VMEM((mine * NBLK, B, B), jnp.float32),
            pltpu.VMEM((order, order), jnp.float32),
            pltpu.VMEM((order, order), jnp.float32),
            pltpu.VMEM((mine, TERMS), jnp.int32),
            pltpu.VMEM((mine, TERMS), jnp.float32),
            pltpu.VMEM((mine, TERMS), jnp.int32),
            pltpu.VMEM((mine, TERMS), jnp.float32),
            pltpu.SMEM((mine, TERMS), jnp.int32),
            pltpu.SMEM((mine, TERMS), jnp.float32),
            pltpu.SMEM((mine, TERMS), jnp.int32),
            pltpu.SMEM((mine, TERMS), jnp.float32),
            pltpu.SemaphoreType.DMA((2, LEVELS + 1, HALVES)),
            pltpu.SemaphoreType.DMA((2, LEVELS, HALVES)),
            pltpu.SemaphoreType.DMA((2, 2, LEVELS, HALVES)),
            pltpu.SemaphoreType.DMA((chan_count, HALVES)),
            pltpu.SemaphoreType.DMA((4,)),
            pltpu.SemaphoreType.DMA((6,)),
            pltpu.SemaphoreType.DMA((NBR,)),
            pltpu.SemaphoreType.DMA((NBR,)),
        ],
        compiler_params=pltpu.CompilerParams(
            collective_id=0, has_side_effects=True, vmem_limit_bytes=LIMIT
        ),
    )(
        eta,
        ham,
        pp_occ[0],
        ph_occ[0],
        jnp.swapaxes(ph_src, 1, 2)[0],
        jnp.swapaxes(coef6j, 1, 2)[0],
    )


def solution(mesh):
    chan_count = mesh.shape["chan"]
    plan = gather_plan if chan_count == LEVELS * 4 else exchange_plan
    return jax.shard_map(
        plan,
        mesh=mesh,
        in_specs=(
            P(("groups", "chan"), None),
            P(("groups", "chan"), None),
            P(("groups", "chan"), None, None),
            P(("groups", "chan"), None, None),
            P(("groups", "chan"), None, None),
            P(("groups", "chan"), None, None),
        ),
        out_specs=P(("groups", "chan"), None),
        check_vma=False,
    )
```

```python
import jax
import jax.numpy as jnp
from jax import lax
from jax.experimental import pallas as pl
from jax.experimental.pallas import tpu as pltpu
from jax.sharding import PartitionSpec as P

B = 128
NBR = 4
K = 8
NBLK = 16
TERMS = NBLK * K
MESH = pl.DeviceIdType.MESH
LIMIT = 60 * 1024 * 1024


def exchange_plan(eta, ham, pp_occ, ph_occ, ph_src, coef6j):
    chan_count = lax.axis_size("chan")
    chan_order = eta.shape[0]
    tile_size = B
    row_tiles = NBR
    tile_count = NBLK
    term_count = tile_count * K
    capacity = max(2, term_count // chan_count)

    def split_tiles(matrix):
        return (
            matrix.reshape(row_tiles, tile_size, row_tiles, tile_size)
            .transpose(0, 2, 1, 3)
            .reshape(tile_count, tile_size, tile_size)
        )

    def join_tiles(tiles):
        return (
            tiles.reshape(row_tiles, row_tiles, tile_size, tile_size)
            .transpose(0, 2, 1, 3)
            .reshape(chan_order, chan_order)
        )

    ref_list = ph_src.reshape(term_count)
    source = ref_list // tile_count
    within = ref_list % tile_count
    lane_ids = jnp.arange(chan_count, dtype=jnp.int32)
    hit_table = (source[:, None] == lane_ids[None, :]).astype(jnp.int32)
    slot_of = jnp.sum(jnp.cumsum(hit_table, axis=0) * hit_table, axis=1) - 1
    place_at = source * capacity + slot_of
    wanted = (
        jnp.full((chan_count * capacity,), -1, jnp.int32)
        .at[place_at]
        .set(within)
        .reshape(chan_count, capacity)
    )
    asked_for = lax.all_to_all(wanted, "chan", split_axis=0, concat_axis=0, tiled=True)
    weights = coef6j.reshape(tile_count, K)
    live = (asked_for >= 0)[:, :, None, None]
    safe_ids = jnp.maximum(asked_for, 0)

    def mix_terms(picked):
        shaped = picked.reshape(tile_count, K, tile_size, tile_size)
        total = jnp.zeros((tile_count, tile_size, tile_size), jnp.float32)
        for term in range(K):
            total = total + shaped[:, term].astype(jnp.float32) * weights[:, term][:, None, None]
        return join_tiles(total.astype(jnp.bfloat16))

    eta_tiles = split_tiles(eta)
    ham_tiles = split_tiles(ham)
    pair_blocks = jnp.stack([eta_tiles, ham_tiles], axis=1)
    outgoing = jnp.where(live[:, :, None], pair_blocks[safe_ids], jnp.zeros((), jnp.bfloat16))
    incoming = lax.all_to_all(outgoing, "chan", split_axis=0, concat_axis=0, tiled=True)
    picked = incoming.reshape(chan_count * capacity, 2, tile_size, tile_size)[place_at]
    ph_eta = mix_terms(picked[:, 0])
    ph_ham = mix_terms(picked[:, 1])
    occ_ph = (ph_occ[0, 0] - ph_occ[0, 1]).astype(jnp.bfloat16)
    z_matrix = jnp.dot(
        ph_eta * occ_ph[None, :], ph_ham, preferred_element_type=jnp.float32
    ) - jnp.dot(ph_ham * occ_ph[None, :], ph_eta, preferred_element_type=jnp.float32)
    back_terms = (
        (split_tiles(z_matrix)[:, None] * weights[:, :, None, None])
        .astype(jnp.bfloat16)
        .reshape(term_count, tile_size, tile_size)
    )
    outgoing_back = (
        jnp.zeros((chan_count * capacity, tile_size, tile_size), jnp.bfloat16)
        .at[place_at]
        .set(back_terms)
        .reshape(chan_count, capacity, tile_size, tile_size)
    )
    returned = lax.all_to_all(outgoing_back, "chan", split_axis=0, concat_axis=0, tiled=True)
    tile_ids = jnp.arange(tile_count, dtype=jnp.int32)
    selector = (asked_for.reshape(chan_count * capacity)[None, :] == tile_ids[:, None]).astype(
        jnp.bfloat16
    )
    ph_term = jnp.dot(
        selector,
        returned.reshape(chan_count * capacity, tile_size * tile_size),
        preferred_element_type=jnp.float32,
    ).reshape(tile_count, tile_size, tile_size)
    occ_pp = (1 - pp_occ[0, 0] - pp_occ[0, 1]).astype(jnp.bfloat16)
    ladder = jnp.dot(eta * occ_pp[None, :], ham, preferred_element_type=jnp.float32) - jnp.dot(
        ham * occ_pp[None, :], eta, preferred_element_type=jnp.float32
    )
    return ladder + join_tiles(ph_term)


LEVELS = 4
HALVES = 2
PER_HALF = NBLK // HALVES
TABLE = 16
CHUNK = PER_HALF * B + TABLE


def flat(values):
    return jnp.concatenate([values[k : k + 1, :] for k in range(K)], axis=1)


def flow_kernel(
    eta_hbm, ham_hbm, pp_occ_hbm, ph_occ_hbm, src_hbm, coef_hbm, out_ref,
    eta_ref, ham_ref, pp_occ_ref, ph_occ_ref, src_ref, coef_ref, packed, eta_full, ham_full, left, right, z_tiles, outbound, inbound,
    src_table, coef_table, pick_table, gain_table, refs, weights, picks, gains,
    send_z, send_x, send_c, recv, local, fetch, send_sum, recv_sum,
):
    group = lax.axis_index("groups")
    me = lax.axis_index("chan")
    level = me // 4
    side = (me // 2) % 2
    core = me % 2
    chan_count = packed.shape[0]
    local_count = chan_count // 2

    def chan_at(lvl, sd, cr):
        return (lvl * 2 + sd) * 2 + cr

    up = chan_at(level + 1, side, core)
    down = chan_at(level - 1, side, core)
    across = chan_at(level, 1 - side, core)
    twin = chan_at(level, side, 1 - core)
    has_up = level < LEVELS - 1
    has_down = level > 0
    mate = level + 1 - 2 * (level % 2)

    barrier = pltpu.get_barrier_semaphore()

    def greet(target):
        pl.semaphore_signal(barrier, inc=1, device_id=(group, target), device_id_type=MESH)

    greet(across)
    greet(twin)

    @pl.when(has_up)
    def _():
        greet(up)

    @pl.when(has_down)
    def _():
        greet(down)

    inputs = (eta_hbm, ham_hbm, src_hbm, coef_hbm, ph_occ_hbm, pp_occ_hbm)
    places = (eta_ref, ham_ref, src_ref, coef_ref, ph_occ_ref, pp_occ_ref)
    fetches = [
        pltpu.make_async_copy(there, here, fetch.at[i])
        for i, (there, here) in enumerate(zip(inputs, places))
    ]
    for copy in fetches:
        copy.start()
    rows = lax.broadcasted_iota(jnp.int32, (B, B), 0)
    cols = lax.broadcasted_iota(jnp.int32, (B, B), 1)

    def tile_rows(block):
        return block // PER_HALF, pl.ds((block % PER_HALF) * B, B)

    for copy in fetches:
        copy.wait()
    for r in range(NBR):
        for s in range(NBR):
            here = (pl.ds(r * B, B), pl.ds(s * B, B))
            if r < s:
                tile = eta_ref[here]
            elif r > s:
                tile = ham_ref[here]
            else:
                tile = jnp.where(rows < cols, eta_ref[here], ham_ref[here])
            half, band = tile_rows(r * NBR + s)
            packed[me, half, band, :] = tile
    coef = flat(coef_ref[...])
    first = coef.astype(jnp.bfloat16)
    rest = coef - first.astype(jnp.float32)
    second = rest.astype(jnp.bfloat16)
    third = (rest - second.astype(jnp.float32)).astype(jnp.bfloat16)
    occ_row = (ph_occ_ref[0:1, :] - ph_occ_ref[1:2, :]).astype(jnp.float32)
    table = jnp.concatenate(
        [
            flat(src_ref[...].astype(jnp.float32)),
            first.astype(jnp.float32),
            second.astype(jnp.float32),
            third.astype(jnp.float32),
            *[occ_row[:, s * B : (s + 1) * B] for s in range(NBR)],
            jnp.zeros((TABLE - 8, B), jnp.float32),
        ],
        axis=0,
    )
    for half in range(HALVES):
        packed[me, half, PER_HALF * B :, :] = table.astype(jnp.bfloat16)

    pl.semaphore_wait(barrier, 2 + has_up.astype(jnp.int32) + has_down.astype(jnp.int32))

    def remote(src, half, sem, target):
        return pltpu.make_async_remote_copy(
            src_ref=packed.at[src, half],
            dst_ref=packed.at[src, half],
            send_sem=sem,
            recv_sem=recv.at[src, half],
            device_id=(group, target),
            device_id_type=MESH,
        )

    def arrived(src, half):
        remote(src, half, send_c.at[0, 0, 0, 0], twin).wait_recv()

    def moves(step, way, lvl, half, act):
        src = chan_at(lvl, side, core)
        if step == 0 or way == 0:
            @pl.when(has_up)
            def _():
                act(remote(src, half, send_z.at[0, step, half], up))
        if step == 0 or way == 1:
            @pl.when(has_down)
            def _():
                act(remote(src, half, send_z.at[1, step, half], down))
        if half >= HALVES // 2 and step == 1:
            @pl.when(lvl != mate)
            def _():
                act(remote(src, half, send_x.at[way, step, half], across))
        else:
            act(remote(src, half, send_x.at[way, step, half], across))
        act(remote(src, half, send_c.at[0, way, step, half], twin))

    def across_moves(step, way, lvl, half, act):
        src = chan_at(lvl, 1 - side, core)
        act(remote(src, half, send_c.at[1, way, step, half], twin))

    def mate_moves(act):
        for half in range(HALVES // 2, HALVES):
            act(remote(across, half, send_z.at[0, LEVELS, half], chan_at(mate, side, core)))

    def each_way(step, action):
        for way in range(2 if step else 1):
            lvl = level - step if way == 0 else level + step
            inside = lvl >= 0 if way == 0 else lvl < LEVELS

            @pl.when(inside)
            def _():
                action(way, lvl)

    def column(step):
        for half in range(HALVES):
            def action(way, lvl):
                if step:
                    arrived(chan_at(lvl, side, core), half)
                moves(step, way, lvl, half, lambda copy: copy.start())

            each_way(step, action)

    def crossing(step, begin=0, end=HALVES):
        for half in range(begin, end):
            def action(way, lvl):
                @pl.when((step != 1) | (half < HALVES // 2) | (lvl != mate))
                def _():
                    arrived(chan_at(lvl, 1 - side, core), half)
                    across_moves(step, way, lvl, half, lambda copy: copy.start())

            each_way(step, action)

    def crossing_mate():
        way = (mate - level + 1) // 2
        for half in range(HALVES // 2, HALVES):
            arrived(chan_at(mate, 1 - side, core), half)
            across_moves(1, way, mate, half, lambda copy: copy.start())

    def expand_mate():
        expand(chan_at(mate, 1 - side, core))
        for half in range(HALVES):
            arrived(chan_at(mate, 1 - side, 1 - core), half)
        expand(chan_at(mate, 1 - side, 1 - core))

    def expand(src):
        base = src * NBLK
        for r in range(NBR):
            for s in range(NBR):
                half, band = tile_rows(r * NBR + s)
                tile = packed[src, half, band, :].astype(jnp.float32)
                flip = tile.T
                if r < s:
                    eta_full[base + r * NBR + s] = tile
                    eta_full[base + s * NBR + r] = -flip
                elif r > s:
                    ham_full[base + r * NBR + s] = tile
                    ham_full[base + s * NBR + r] = flip
                else:
                    zero = jnp.zeros_like(tile)
                    eta_full[base + r * NBR + s] = jnp.where(
                        rows < cols, tile, jnp.where(rows > cols, -flip, zero)
                    )
                    ham_full[base + r * NBR + s] = jnp.where(rows >= cols, tile, flip)

    def expand_all(step, members):
        ways = 2 if step else 1

        @pl.loop(0, ways * len(members))
        def _(turn):
            way = turn % ways
            lvl = level + (2 * way - 1) * step

            facing = members[0][0] if len(members) == 1 else turn // ways
            later = (facing != side) & (lvl == mate)

            @pl.when((lvl >= 0) & (lvl < LEVELS) & jnp.logical_not(later))
            def _():
                place = members[0] if len(members) == 1 else turn // ways
                if len(members) == 1:
                    sd, cr = place
                    src = chan_at(lvl, sd, cr)
                else:
                    src = chan_at(lvl, place, 1 - core)
                    for half in range(HALVES):
                        arrived(src, half)
                expand(src)

    def expand_twin(step):
        expand_all(step, (0, 1))

    column(0)
    occ = (1 - pp_occ_ref[0:1, :] - pp_occ_ref[1:2, :]).astype(jnp.bfloat16)
    for r in range(NBR):
        band = pl.ds(r * B, B)
        out_ref[band, :] = jnp.dot(
            eta_ref[band, :] * occ, ham_ref[...], preferred_element_type=jnp.float32
        ) - jnp.dot(ham_ref[band, :] * occ, eta_ref[...], preferred_element_type=jnp.float32)
    expand_all(0, ((side, core),))
    for step in range(1, LEVELS):
        column(step)
        if step == LEVELS - 1:
            mate_moves(lambda copy: copy.start())
        crossing(step - 1)
        expand_all(step, ((side, core),))
        expand_all(step - 1, ((1 - side, core),))
        if step >= 2:
            expand_twin(step - 2)
    crossing(LEVELS - 1, 0, 1)
    for q in range(local_count):
        table = packed[2 * q + core, 0, PER_HALF * B :, :].astype(jnp.float32)
        src_table[q : q + 1, :] = jnp.clip(
            table[0:1, :].astype(jnp.int32), 0, chan_count * NBLK - 1
        )
        coef_table[q : q + 1, :] = table[1:2, :] + (table[2:3, :] + table[3:4, :])
    loads = [
        pltpu.make_async_copy(src_table, refs, local.at[0]),
        pltpu.make_async_copy(coef_table, weights, local.at[1]),
    ]
    for load in loads:
        load.start()
    named = src_table[...]
    factor = coef_table[...]
    lanes = lax.broadcasted_iota(jnp.int32, named.shape, 1)
    found = jnp.zeros(named.shape, jnp.int32)
    gain = jnp.zeros(named.shape, jnp.float32)
    for place in range(2 * NBLK):
        owner = me if place < NBLK else twin
        hit = named == owner * NBLK + place % NBLK
        tile = jnp.max(jnp.where(hit, lanes % NBLK, 0), axis=1, keepdims=True)
        scale = jnp.sum(jnp.where(hit, factor, 0.0), axis=1, keepdims=True)
        found = jnp.where(lanes == place, tile, found)
        gain = jnp.where(lanes == place, scale, gain)
    pick_table[...] = found
    gain_table[...] = gain
    more = [
        pltpu.make_async_copy(pick_table, picks, local.at[2]),
        pltpu.make_async_copy(gain_table, gains, local.at[3]),
    ]
    for load in more:
        load.start()
    crossing(LEVELS - 1, 1, HALVES)
    crossing_mate()
    expand_twin(LEVELS - 2)
    expand_all(LEVELS - 1, ((1 - side, core),))
    expand_twin(LEVELS - 1)
    expand_mate()

    for load in loads:
        load.wait()

    part_rows = B // 2
    order = NBR * B

    @pl.loop(0, local_count)
    def _(q):
        @pl.loop(0, NBR)
        def _(r):
            for s in range(NBR):
                scale = packed[2 * q + core, 0, PER_HALF * B :, :][4 + s : 5 + s, :]
                for part in range(2):
                    span = pl.ds(part * part_rows, part_rows)
                    total_eta = jnp.zeros((part_rows, B), jnp.float32)
                    total_ham = jnp.zeros((part_rows, B), jnp.float32)
                    for term in range(K):
                        at = term * NBLK + r * NBR + s
                        which = refs[q, at]
                        weight = weights[q, at]
                        total_eta += eta_full[which, span, :] * weight
                        total_ham += ham_full[which, span, :] * weight
                    start = pl.multiple_of(r * B + part * part_rows, part_rows)
                    lane = slice(s * B, (s + 1) * B)
                    beyond = slice(order + s * B, order + (s + 1) * B)
                    mixed_eta = total_eta.astype(jnp.bfloat16)
                    mixed_ham = total_ham.astype(jnp.bfloat16)
                    left[pl.ds(start, part_rows), lane] = mixed_eta * scale
                    left[pl.ds(start, part_rows), beyond] = -(mixed_ham * scale)
                    right[pl.ds(start, part_rows), lane] = mixed_ham
                    right[pl.ds(order + start, part_rows), lane] = mixed_eta

        for pair in range(NBR // 2):
            lane = slice(2 * pair * B, 2 * (pair + 1) * B)
            slab = jnp.dot(left[...], right[:, lane], preferred_element_type=jnp.float32)
            for r in range(NBR):
                for s in range(2):
                    z_tiles[q * NBLK + r * NBR + 2 * pair + s] = slab[
                        r * B : (r + 1) * B, s * B : (s + 1) * B
                    ]

    for load in more:
        load.wait()

    def sum_back(first, target, r, keep):
        for s in range(NBR):
            for part in range(2):
                span = pl.ds(part * part_rows, part_rows)
                total = jnp.zeros((part_rows, B), jnp.float32)
                for q in range(local_count):
                    at = first + r * NBR + s
                    tile = z_tiles[q * NBLK + picks[q, at], span, :]
                    total += tile * gains[q, at]
                here = (
                    slice(r * B + part * part_rows, r * B + (part + 1) * part_rows),
                    slice(s * B, (s + 1) * B),
                )
                target[here] = target[here] + total if keep else total

    swaps = []
    for r in range(NBR):
        sum_back(NBLK, outbound, r, False)
        swap = pltpu.make_async_remote_copy(
            src_ref=outbound.at[pl.ds(r * B, B)],
            dst_ref=inbound.at[pl.ds(r * B, B)],
            send_sem=send_sum.at[r],
            recv_sem=recv_sum.at[r],
            device_id=(group, twin),
            device_id_type=MESH,
        )
        swap.start()
        swaps.append(swap)
    for r in range(NBR):
        sum_back(0, out_ref, r, True)

    for step in range(LEVELS):
        for half in range(HALVES):
            each_way(step, lambda way, lvl: moves(step, way, lvl, half, lambda copy: copy.wait_send()))
            each_way(
                step, lambda way, lvl: across_moves(step, way, lvl, half, lambda copy: copy.wait_send())
            )
    mate_moves(lambda copy: copy.wait_send())
    for r, swap in enumerate(swaps):
        swap.wait()
        band = slice(r * B, (r + 1) * B)
        out_ref[band, :] += inbound[band, :]


def gather_plan(eta, ham, pp_occ, ph_occ, ph_src, coef6j):
    chan_count = lax.axis_size("chan")
    order = eta.shape[0]
    vmem = pl.BlockSpec(memory_space=pltpu.VMEM)
    blocks = chan_count * NBLK
    mine = chan_count // 2
    return pl.pallas_call(
        flow_kernel,
        out_shape=jax.ShapeDtypeStruct((order, order), jnp.float32),
        in_specs=[pl.BlockSpec(memory_space=pl.ANY)] * 6,
        out_specs=vmem,
        scratch_shapes=[
            pltpu.VMEM((order, order), jnp.bfloat16),
            pltpu.VMEM((order, order), jnp.bfloat16),
            pltpu.VMEM((2, order), jnp.int32),
            pltpu.VMEM((2, order), jnp.int32),
            pltpu.VMEM((K, NBLK), jnp.int32),
            pltpu.VMEM((K, NBLK), jnp.float32),
            pltpu.VMEM((chan_count, HALVES, CHUNK, B), jnp.bfloat16),
            pltpu.VMEM((blocks, B, B), jnp.float32),
            pltpu.VMEM((blocks, B, B), jnp.float32),
            pltpu.VMEM((order, 2 * order), jnp.bfloat16),
            pltpu.VMEM((2 * order, order), jnp.bfloat16),
            pltpu.VMEM((mine * NBLK, B, B), jnp.float32),
            pltpu.VMEM((order, order), jnp.float32),
            pltpu.VMEM((order, order), jnp.float32),
            pltpu.VMEM((mine, TERMS), jnp.int32),
            pltpu.VMEM((mine, TERMS), jnp.float32),
            pltpu.VMEM((mine, TERMS), jnp.int32),
            pltpu.VMEM((mine, TERMS), jnp.float32),
            pltpu.SMEM((mine, TERMS), jnp.int32),
            pltpu.SMEM((mine, TERMS), jnp.float32),
            pltpu.SMEM((mine, TERMS), jnp.int32),
            pltpu.SMEM((mine, TERMS), jnp.float32),
            pltpu.SemaphoreType.DMA((2, LEVELS + 1, HALVES)),
            pltpu.SemaphoreType.DMA((2, LEVELS, HALVES)),
            pltpu.SemaphoreType.DMA((2, 2, LEVELS, HALVES)),
            pltpu.SemaphoreType.DMA((chan_count, HALVES)),
            pltpu.SemaphoreType.DMA((4,)),
            pltpu.SemaphoreType.DMA((6,)),
            pltpu.SemaphoreType.DMA((NBR,)),
            pltpu.SemaphoreType.DMA((NBR,)),
        ],
        compiler_params=pltpu.CompilerParams(
            collective_id=0, has_side_effects=True, vmem_limit_bytes=LIMIT
        ),
    )(
        eta,
        ham,
        pp_occ[0],
        ph_occ[0],
        jnp.swapaxes(ph_src, 1, 2)[0],
        jnp.swapaxes(coef6j, 1, 2)[0],
    )


def solution(mesh):
    chan_count = mesh.shape["chan"]
    plan = gather_plan if chan_count == LEVELS * 4 else exchange_plan
    return jax.shard_map(
        plan,
        mesh=mesh,
        in_specs=(
            P(("groups", "chan"), None),
            P(("groups", "chan"), None),
            P(("groups", "chan"), None, None),
            P(("groups", "chan"), None, None),
            P(("groups", "chan"), None, None),
            P(("groups", "chan"), None, None),
        ),
        out_specs=P(("groups", "chan"), None),
        check_vma=False,
    )
```

```python
import jax
import jax.numpy as jnp
from jax import lax
from jax.experimental import pallas as pl
from jax.experimental.pallas import tpu as pltpu
from jax.sharding import PartitionSpec as P

B = 128
NBR = 4
K = 8
NBLK = 16
TERMS = NBLK * K
MESH = pl.DeviceIdType.MESH
LIMIT = 60 * 1024 * 1024


def exchange_plan(eta, ham, pp_occ, ph_occ, ph_src, coef6j):
    chan_count = lax.axis_size("chan")
    chan_order = eta.shape[0]
    tile_size = B
    row_tiles = NBR
    tile_count = NBLK
    term_count = tile_count * K
    capacity = max(2, term_count // chan_count)

    def split_tiles(matrix):
        return (
            matrix.reshape(row_tiles, tile_size, row_tiles, tile_size)
            .transpose(0, 2, 1, 3)
            .reshape(tile_count, tile_size, tile_size)
        )

    def join_tiles(tiles):
        return (
            tiles.reshape(row_tiles, row_tiles, tile_size, tile_size)
            .transpose(0, 2, 1, 3)
            .reshape(chan_order, chan_order)
        )

    ref_list = ph_src.reshape(term_count)
    source = ref_list // tile_count
    within = ref_list % tile_count
    lane_ids = jnp.arange(chan_count, dtype=jnp.int32)
    hit_table = (source[:, None] == lane_ids[None, :]).astype(jnp.int32)
    slot_of = jnp.sum(jnp.cumsum(hit_table, axis=0) * hit_table, axis=1) - 1
    place_at = source * capacity + slot_of
    wanted = (
        jnp.full((chan_count * capacity,), -1, jnp.int32)
        .at[place_at]
        .set(within)
        .reshape(chan_count, capacity)
    )
    asked_for = lax.all_to_all(wanted, "chan", split_axis=0, concat_axis=0, tiled=True)
    weights = coef6j.reshape(tile_count, K)
    live = (asked_for >= 0)[:, :, None, None]
    safe_ids = jnp.maximum(asked_for, 0)

    def mix_terms(picked):
        shaped = picked.reshape(tile_count, K, tile_size, tile_size)
        total = jnp.zeros((tile_count, tile_size, tile_size), jnp.float32)
        for term in range(K):
            total = total + shaped[:, term].astype(jnp.float32) * weights[:, term][:, None, None]
        return join_tiles(total.astype(jnp.bfloat16))

    eta_tiles = split_tiles(eta)
    ham_tiles = split_tiles(ham)
    pair_blocks = jnp.stack([eta_tiles, ham_tiles], axis=1)
    outgoing = jnp.where(live[:, :, None], pair_blocks[safe_ids], jnp.zeros((), jnp.bfloat16))
    incoming = lax.all_to_all(outgoing, "chan", split_axis=0, concat_axis=0, tiled=True)
    picked = incoming.reshape(chan_count * capacity, 2, tile_size, tile_size)[place_at]
    ph_eta = mix_terms(picked[:, 0])
    ph_ham = mix_terms(picked[:, 1])
    occ_ph = (ph_occ[0, 0] - ph_occ[0, 1]).astype(jnp.bfloat16)
    z_matrix = jnp.dot(
        ph_eta * occ_ph[None, :], ph_ham, preferred_element_type=jnp.float32
    ) - jnp.dot(ph_ham * occ_ph[None, :], ph_eta, preferred_element_type=jnp.float32)
    back_terms = (
        (split_tiles(z_matrix)[:, None] * weights[:, :, None, None])
        .astype(jnp.bfloat16)
        .reshape(term_count, tile_size, tile_size)
    )
    outgoing_back = (
        jnp.zeros((chan_count * capacity, tile_size, tile_size), jnp.bfloat16)
        .at[place_at]
        .set(back_terms)
        .reshape(chan_count, capacity, tile_size, tile_size)
    )
    returned = lax.all_to_all(outgoing_back, "chan", split_axis=0, concat_axis=0, tiled=True)
    tile_ids = jnp.arange(tile_count, dtype=jnp.int32)
    selector = (asked_for.reshape(chan_count * capacity)[None, :] == tile_ids[:, None]).astype(
        jnp.bfloat16
    )
    ph_term = jnp.dot(
        selector,
        returned.reshape(chan_count * capacity, tile_size * tile_size),
        preferred_element_type=jnp.float32,
    ).reshape(tile_count, tile_size, tile_size)
    occ_pp = (1 - pp_occ[0, 0] - pp_occ[0, 1]).astype(jnp.bfloat16)
    ladder = jnp.dot(eta * occ_pp[None, :], ham, preferred_element_type=jnp.float32) - jnp.dot(
        ham * occ_pp[None, :], eta, preferred_element_type=jnp.float32
    )
    return ladder + join_tiles(ph_term)


LEVELS = 4
HALVES = 2
PER_HALF = NBLK // HALVES
TABLE = 16
CHUNK = PER_HALF * B + TABLE


def flat(values):
    return jnp.concatenate([values[k : k + 1, :] for k in range(K)], axis=1)


def flow_kernel(
    eta_hbm, ham_hbm, pp_occ_hbm, ph_occ_hbm, src_hbm, coef_hbm, out_ref,
    eta_ref, ham_ref, pp_occ_ref, ph_occ_ref, src_ref, coef_ref, packed, eta_full, ham_full, left, right, z_tiles, outbound, inbound,
    src_table, coef_table, pick_table, gain_table, refs, weights, picks, gains,
    send_z, send_x, send_c, recv, local, fetch, send_sum, recv_sum,
):
    group = lax.axis_index("groups")
    me = lax.axis_index("chan")
    level = me // 4
    side = (me // 2) % 2
    core = me % 2
    chan_count = packed.shape[0]
    local_count = chan_count // 2

    def chan_at(lvl, sd, cr):
        return (lvl * 2 + sd) * 2 + cr

    up = chan_at(level + 1, side, core)
    down = chan_at(level - 1, side, core)
    across = chan_at(level, 1 - side, core)
    twin = chan_at(level, side, 1 - core)
    has_up = level < LEVELS - 1
    has_down = level > 0
    mate = level + 1 - 2 * (level % 2)

    barrier = pltpu.get_barrier_semaphore()

    def greet(target):
        pl.semaphore_signal(barrier, inc=1, device_id=(group, target), device_id_type=MESH)

    greet(across)
    greet(twin)

    @pl.when(has_up)
    def _():
        greet(up)

    @pl.when(has_down)
    def _():
        greet(down)

    inputs = (eta_hbm, ham_hbm, src_hbm, coef_hbm, ph_occ_hbm, pp_occ_hbm)
    places = (eta_ref, ham_ref, src_ref, coef_ref, ph_occ_ref, pp_occ_ref)
    fetches = [
        pltpu.make_async_copy(there, here, fetch.at[i])
        for i, (there, here) in enumerate(zip(inputs, places))
    ]
    for copy in fetches:
        copy.start()
    rows = lax.broadcasted_iota(jnp.int32, (B, B), 0)
    cols = lax.broadcasted_iota(jnp.int32, (B, B), 1)

    def tile_rows(block):
        return block // PER_HALF, pl.ds((block % PER_HALF) * B, B)

    for copy in fetches:
        copy.wait()
    for r in range(NBR):
        for s in range(NBR):
            here = (pl.ds(r * B, B), pl.ds(s * B, B))
            if r < s:
                tile = eta_ref[here]
            elif r > s:
                tile = ham_ref[here]
            else:
                tile = jnp.where(rows < cols, eta_ref[here], ham_ref[here])
            half, band = tile_rows(r * NBR + s)
            packed[me, half, band, :] = tile
    coef = flat(coef_ref[...])
    first = coef.astype(jnp.bfloat16)
    rest = coef - first.astype(jnp.float32)
    second = rest.astype(jnp.bfloat16)
    third = (rest - second.astype(jnp.float32)).astype(jnp.bfloat16)
    occ_row = (ph_occ_ref[0:1, :] - ph_occ_ref[1:2, :]).astype(jnp.float32)
    table = jnp.concatenate(
        [
            flat(src_ref[...].astype(jnp.float32)),
            first.astype(jnp.float32),
            second.astype(jnp.float32),
            third.astype(jnp.float32),
            *[occ_row[:, s * B : (s + 1) * B] for s in range(NBR)],
            jnp.zeros((TABLE - 8, B), jnp.float32),
        ],
        axis=0,
    )
    for half in range(HALVES):
        packed[me, half, PER_HALF * B :, :] = table.astype(jnp.bfloat16)

    pl.semaphore_wait(barrier, 2 + has_up.astype(jnp.int32) + has_down.astype(jnp.int32))

    def remote(src, half, sem, target):
        return pltpu.make_async_remote_copy(
            src_ref=packed.at[src, half],
            dst_ref=packed.at[src, half],
            send_sem=sem,
            recv_sem=recv.at[src, half],
            device_id=(group, target),
            device_id_type=MESH,
        )

    def arrived(src, half):
        remote(src, half, send_c.at[0, 0, 0, 0], twin).wait_recv()

    def moves(step, way, lvl, half, act):
        src = chan_at(lvl, side, core)
        if step == 0 or way == 0:
            @pl.when(has_up)
            def _():
                act(remote(src, half, send_z.at[0, step, half], up))
        if step == 0 or way == 1:
            @pl.when(has_down)
            def _():
                act(remote(src, half, send_z.at[1, step, half], down))
        if half >= HALVES // 2 and step == 1:
            @pl.when(lvl != mate)
            def _():
                act(remote(src, half, send_x.at[way, step, half], across))
        else:
            act(remote(src, half, send_x.at[way, step, half], across))
        act(remote(src, half, send_c.at[0, way, step, half], twin))

    def across_moves(step, way, lvl, half, act):
        src = chan_at(lvl, 1 - side, core)
        act(remote(src, half, send_c.at[1, way, step, half], twin))

    def mate_moves(act):
        for half in range(HALVES // 2, HALVES):
            act(remote(across, half, send_z.at[0, LEVELS, half], chan_at(mate, side, core)))

    def each_way(step, action):
        for way in range(2 if step else 1):
            lvl = level - step if way == 0 else level + step
            inside = lvl >= 0 if way == 0 else lvl < LEVELS

            @pl.when(inside)
            def _():
                action(way, lvl)

    def column(step):
        for half in range(HALVES):
            def action(way, lvl):
                if step:
                    arrived(chan_at(lvl, side, core), half)
                moves(step, way, lvl, half, lambda copy: copy.start())

            each_way(step, action)

    def crossing(step, begin=0, end=HALVES):
        for half in range(begin, end):
            def action(way, lvl):
                @pl.when((step != 1) | (half < HALVES // 2) | (lvl != mate))
                def _():
                    arrived(chan_at(lvl, 1 - side, core), half)
                    across_moves(step, way, lvl, half, lambda copy: copy.start())

            each_way(step, action)

    def crossing_mate():
        way = (mate - level + 1) // 2
        for half in range(HALVES // 2, HALVES):
            arrived(chan_at(mate, 1 - side, core), half)
            across_moves(1, way, mate, half, lambda copy: copy.start())

    def expand_mate():
        expand(chan_at(mate, 1 - side, core))
        for half in range(HALVES):
            arrived(chan_at(mate, 1 - side, 1 - core), half)
        expand(chan_at(mate, 1 - side, 1 - core))

    def expand(src):
        base = src * NBLK
        for r in range(NBR):
            for s in range(NBR):
                half, band = tile_rows(r * NBR + s)
                tile = packed[src, half, band, :].astype(jnp.float32)
                flip = tile.T
                if r < s:
                    eta_full[base + r * NBR + s] = tile
                    eta_full[base + s * NBR + r] = -flip
                elif r > s:
                    ham_full[base + r * NBR + s] = tile
                    ham_full[base + s * NBR + r] = flip
                else:
                    zero = jnp.zeros_like(tile)
                    eta_full[base + r * NBR + s] = jnp.where(
                        rows < cols, tile, jnp.where(rows > cols, -flip, zero)
                    )
                    ham_full[base + r * NBR + s] = jnp.where(rows >= cols, tile, flip)

    def expand_all(step, members):
        ways = 2 if step else 1

        @pl.loop(0, ways * len(members))
        def _(turn):
            way = turn % ways
            lvl = level + (2 * way - 1) * step

            facing = members[0][0] if len(members) == 1 else turn // ways
            later = (facing != side) & (lvl == mate)

            @pl.when((lvl >= 0) & (lvl < LEVELS) & jnp.logical_not(later))
            def _():
                place = members[0] if len(members) == 1 else turn // ways
                if len(members) == 1:
                    sd, cr = place
                    src = chan_at(lvl, sd, cr)
                else:
                    src = chan_at(lvl, place, 1 - core)
                    for half in range(HALVES):
                        arrived(src, half)
                expand(src)

    def expand_twin(step):
        expand_all(step, (0, 1))

    column(0)
    occ = (1 - pp_occ_ref[0:1, :] - pp_occ_ref[1:2, :]).astype(jnp.bfloat16)
    for r in range(NBR):
        band = pl.ds(r * B, B)
        out_ref[band, :] = jnp.dot(
            eta_ref[band, :] * occ, ham_ref[...], preferred_element_type=jnp.float32
        ) - jnp.dot(ham_ref[band, :] * occ, eta_ref[...], preferred_element_type=jnp.float32)
    expand_all(0, ((side, core),))
    for step in range(1, LEVELS):
        column(step)
        if step == LEVELS - 1:
            mate_moves(lambda copy: copy.start())
        crossing(step - 1)
        expand_all(step, ((side, core),))
        expand_all(step - 1, ((1 - side, core),))
        if step >= 2:
            expand_twin(step - 2)
    crossing(LEVELS - 1, 0, 1)
    for q in range(local_count):
        table = packed[2 * q + core, 0, PER_HALF * B :, :].astype(jnp.float32)
        src_table[q : q + 1, :] = jnp.clip(
            table[0:1, :].astype(jnp.int32), 0, chan_count * NBLK - 1
        )
        coef_table[q : q + 1, :] = table[1:2, :] + (table[2:3, :] + table[3:4, :])
    loads = [
        pltpu.make_async_copy(src_table, refs, local.at[0]),
        pltpu.make_async_copy(coef_table, weights, local.at[1]),
    ]
    for load in loads:
        load.start()
    named = src_table[...]
    factor = coef_table[...]
    lanes = lax.broadcasted_iota(jnp.int32, named.shape, 1)
    found = jnp.zeros(named.shape, jnp.int32)
    gain = jnp.zeros(named.shape, jnp.float32)
    for place in range(2 * NBLK):
        owner = me if place < NBLK else twin
        hit = named == owner * NBLK + place % NBLK
        tile = jnp.max(jnp.where(hit, lanes % NBLK, 0), axis=1, keepdims=True)
        scale = jnp.sum(jnp.where(hit, factor, 0.0), axis=1, keepdims=True)
        found = jnp.where(lanes == place, tile, found)
        gain = jnp.where(lanes == place, scale, gain)
    pick_table[...] = found
    gain_table[...] = gain
    more = [
        pltpu.make_async_copy(pick_table, picks, local.at[2]),
        pltpu.make_async_copy(gain_table, gains, local.at[3]),
    ]
    for load in more:
        load.start()
    crossing(LEVELS - 1, 1, HALVES)
    crossing_mate()
    expand_twin(LEVELS - 2)
    expand_all(LEVELS - 1, ((1 - side, core),))
    expand_twin(LEVELS - 1)
    expand_mate()

    for load in loads:
        load.wait()

    part_rows = B
    order = NBR * B

    @pl.loop(0, local_count)
    def _(q):
        @pl.loop(0, NBR)
        def _(r):
            for s in range(NBR):
                scale = packed[2 * q + core, 0, PER_HALF * B :, :][4 + s : 5 + s, :]
                for part in range(1):
                    span = pl.ds(part * part_rows, part_rows)
                    total_eta = jnp.zeros((part_rows, B), jnp.float32)
                    total_ham = jnp.zeros((part_rows, B), jnp.float32)
                    for term in range(K):
                        at = term * NBLK + r * NBR + s
                        which = refs[q, at]
                        weight = weights[q, at]
                        total_eta += eta_full[which, span, :] * weight
                        total_ham += ham_full[which, span, :] * weight
                    start = pl.multiple_of(r * B + part * part_rows, part_rows)
                    lane = slice(s * B, (s + 1) * B)
                    beyond = slice(order + s * B, order + (s + 1) * B)
                    mixed_eta = total_eta.astype(jnp.bfloat16)
                    mixed_ham = total_ham.astype(jnp.bfloat16)
                    left[pl.ds(start, part_rows), lane] = mixed_eta * scale
                    left[pl.ds(start, part_rows), beyond] = -(mixed_ham * scale)
                    right[pl.ds(start, part_rows), lane] = mixed_ham
                    right[pl.ds(order + start, part_rows), lane] = mixed_eta

        for pair in range(NBR // 2):
            lane = slice(2 * pair * B, 2 * (pair + 1) * B)
            slab = jnp.dot(left[...], right[:, lane], preferred_element_type=jnp.float32)
            for r in range(NBR):
                for s in range(2):
                    z_tiles[q * NBLK + r * NBR + 2 * pair + s] = slab[
                        r * B : (r + 1) * B, s * B : (s + 1) * B
                    ]

    for load in more:
        load.wait()

    def sum_back(first, target, r, keep):
        for s in range(NBR):
            for part in range(1):
                span = pl.ds(part * part_rows, part_rows)
                total = jnp.zeros((part_rows, B), jnp.float32)
                for q in range(local_count):
                    at = first + r * NBR + s
                    tile = z_tiles[q * NBLK + picks[q, at], span, :]
                    total += tile * gains[q, at]
                here = (
                    slice(r * B + part * part_rows, r * B + (part + 1) * part_rows),
                    slice(s * B, (s + 1) * B),
                )
                target[here] = target[here] + total if keep else total

    swaps = []
    for r in range(NBR):
        sum_back(NBLK, outbound, r, False)
        swap = pltpu.make_async_remote_copy(
            src_ref=outbound.at[pl.ds(r * B, B)],
            dst_ref=inbound.at[pl.ds(r * B, B)],
            send_sem=send_sum.at[r],
            recv_sem=recv_sum.at[r],
            device_id=(group, twin),
            device_id_type=MESH,
        )
        swap.start()
        swaps.append(swap)
    for r in range(NBR):
        sum_back(0, out_ref, r, True)

    for step in range(LEVELS):
        for half in range(HALVES):
            each_way(step, lambda way, lvl: moves(step, way, lvl, half, lambda copy: copy.wait_send()))
            each_way(
                step, lambda way, lvl: across_moves(step, way, lvl, half, lambda copy: copy.wait_send())
            )
    mate_moves(lambda copy: copy.wait_send())
    for r, swap in enumerate(swaps):
        swap.wait()
        band = slice(r * B, (r + 1) * B)
        out_ref[band, :] += inbound[band, :]


def gather_plan(eta, ham, pp_occ, ph_occ, ph_src, coef6j):
    chan_count = lax.axis_size("chan")
    order = eta.shape[0]
    vmem = pl.BlockSpec(memory_space=pltpu.VMEM)
    blocks = chan_count * NBLK
    mine = chan_count // 2
    return pl.pallas_call(
        flow_kernel,
        out_shape=jax.ShapeDtypeStruct((order, order), jnp.float32),
        in_specs=[pl.BlockSpec(memory_space=pl.ANY)] * 6,
        out_specs=vmem,
        scratch_shapes=[
            pltpu.VMEM((order, order), jnp.bfloat16),
            pltpu.VMEM((order, order), jnp.bfloat16),
            pltpu.VMEM((2, order), jnp.int32),
            pltpu.VMEM((2, order), jnp.int32),
            pltpu.VMEM((K, NBLK), jnp.int32),
            pltpu.VMEM((K, NBLK), jnp.float32),
            pltpu.VMEM((chan_count, HALVES, CHUNK, B), jnp.bfloat16),
            pltpu.VMEM((blocks, B, B), jnp.float32),
            pltpu.VMEM((blocks, B, B), jnp.float32),
            pltpu.VMEM((order, 2 * order), jnp.bfloat16),
            pltpu.VMEM((2 * order, order), jnp.bfloat16),
            pltpu.VMEM((mine * NBLK, B, B), jnp.float32),
            pltpu.VMEM((order, order), jnp.float32),
            pltpu.VMEM((order, order), jnp.float32),
            pltpu.VMEM((mine, TERMS), jnp.int32),
            pltpu.VMEM((mine, TERMS), jnp.float32),
            pltpu.VMEM((mine, TERMS), jnp.int32),
            pltpu.VMEM((mine, TERMS), jnp.float32),
            pltpu.SMEM((mine, TERMS), jnp.int32),
            pltpu.SMEM((mine, TERMS), jnp.float32),
            pltpu.SMEM((mine, TERMS), jnp.int32),
            pltpu.SMEM((mine, TERMS), jnp.float32),
            pltpu.SemaphoreType.DMA((2, LEVELS + 1, HALVES)),
            pltpu.SemaphoreType.DMA((2, LEVELS, HALVES)),
            pltpu.SemaphoreType.DMA((2, 2, LEVELS, HALVES)),
            pltpu.SemaphoreType.DMA((chan_count, HALVES)),
            pltpu.SemaphoreType.DMA((4,)),
            pltpu.SemaphoreType.DMA((6,)),
            pltpu.SemaphoreType.DMA((NBR,)),
            pltpu.SemaphoreType.DMA((NBR,)),
        ],
        compiler_params=pltpu.CompilerParams(
            collective_id=0, has_side_effects=True, vmem_limit_bytes=LIMIT
        ),
    )(
        eta,
        ham,
        pp_occ[0],
        ph_occ[0],
        jnp.swapaxes(ph_src, 1, 2)[0],
        jnp.swapaxes(coef6j, 1, 2)[0],
    )


def solution(mesh):
    chan_count = mesh.shape["chan"]
    plan = gather_plan if chan_count == LEVELS * 4 else exchange_plan
    return jax.shard_map(
        plan,
        mesh=mesh,
        in_specs=(
            P(("groups", "chan"), None),
            P(("groups", "chan"), None),
            P(("groups", "chan"), None, None),
            P(("groups", "chan"), None, None),
            P(("groups", "chan"), None, None),
            P(("groups", "chan"), None, None),
        ),
        out_specs=P(("groups", "chan"), None),
        check_vma=False,
    )
```
